256 devices in a mesh: batch: 16 (over x, y), layer: 16 (over z, core).
Axes of the slice: x: 4, y: 4, z: 8, core: 2. Of those that a mesh axis runs over, the one named last changes fastest.
Arguments:
- inputs: float32 [256, 4096], P(None, 'batch'), parts along dimension 1, may hold values from -6 to 6
- guess: float32 [16, 256, 4096], P('layer', None, 'batch'), parts along dimension 2, may hold values from -6 to 6
- weights: bfloat16 [64, 256, 2304], P('layer'), may hold values from -0.125 to 0.125
Outputs:
- states: float32 [64, 256, 4096], P('layer', None, 'batch'), parts along dimension 2
The draws below stay inside these ranges and needn't reach their ends.
There are 16 independent parts, one for each index of `batch`. The reference program is written for one: setup_inputs(seed, part) draws one part's arguments, and reference() takes and returns one part's arrays. A program takes and returns all parts, laid end to end along the dimension named above; an argument that names none is the same for every part. Nothing has to cross between parts.
All inputs are finite; a program needn't handle non-finite values.
Results may differ from the reference program's by a relative error of at most 0.01.
Values may be sent and summed in bfloat16 or wider, within the bound.
No kernel may reach another device: no remote copies, remote signals or barrier semaphores. Data moves between devices by JAX's collectives and lax.ppermute only.
A program may use at most 64 MiB of HBM per device.

```python
import jax
import jax.numpy as jnp

CHANNELS = 256
HEIGHT = 16
WIDTH = 16
COARSEN = 4
CELLS = 256
LAYERS = 64
POINTS = 16


def level_of(own_key, dims, split, least, high):
    level, own = 1.0, jax.random.fold_in(own_key, 6)
    for dim, shards_of in split:
        steps = jnp.exp(jax.random.uniform(jax.random.fold_in(own, dim), (shards_of,), jnp.float32, least / len(split), high / len(split)))
        level = level * jnp.repeat(steps, dims[dim] // shards_of).reshape([-1 if axis == dim else 1 for axis in range(len(dims))])
    return level


def normal_values(own_key, dims, width, limit, cuts=(), dtype=jnp.bfloat16):
    loudness = level_of(own_key, dims, cuts, -0.22, 0.18) if cuts else 1.0
    entries = jax.random.normal(own_key, dims, jnp.float32) * width * loudness
    return jnp.minimum(jnp.maximum(entries, -limit), limit).astype(dtype)


def setup_inputs(seed: int = 0, part: int = 0) -> dict:
    seeds = jax.random.split(jax.random.key(seed), 4)
    own_keys = jax.random.split(jax.random.fold_in(seeds[3], part), 4)
    inputs = normal_values(own_keys[0], (CHANNELS, CELLS), 1.0, 6.0, (), jnp.float32)
    guess = normal_values(own_keys[1], (POINTS, CHANNELS, CELLS), 1.0, 6.0, ((0, 16),), jnp.float32)
    weights = normal_values(seeds[2], (LAYERS, CHANNELS, 9 * CHANNELS), (9 * CHANNELS) ** -0.5, 0.125, ((0, 16),))
    return {"inputs": inputs, "guess": guess, "weights": weights}


def convolve(weight, state):
    chans = state.shape[0]
    grid = state.astype(jnp.bfloat16).reshape(chans, HEIGHT, WIDTH)
    padded = jnp.pad(grid, ((0, 0), (1, 1), (1, 1)))
    pieces = [padded[:, 1 + rowoff:1 + rowoff + HEIGHT, 1 + coloff:1 + coloff + WIDTH] for rowoff in (-1, 0, 1) for coloff in (-1, 0, 1)]
    stacked = jnp.concatenate(pieces, 0).reshape(9 * chans, HEIGHT * WIDTH)
    return jnp.dot(weight, stacked, preferred_element_type=jnp.float32)


def advance(weight, state, factor):
    return state + factor * jnp.tanh(convolve(weight, state))


many = jax.vmap(advance, in_axes=(0, 0, None))


def reference(inputs, guess, weights):
    points = guess.shape[0]
    blocks = weights.reshape(points, COARSEN, weights.shape[1], weights.shape[2])
    firsts = blocks[:, 0]

    def fine_sweep(lefts):
        result = []
        state = lefts
        for inner in range(COARSEN - 1):
            state = many(blocks[:, inner], state, 0.25)
            result.append(state)
        return result

    def shifted(values):
        return jnp.concatenate([inputs[None], values[:-1]], 0)

    position = jnp.arange(points)[:, None, None] % COARSEN
    lefts = jnp.concatenate([inputs[None], guess[1:]], 0)
    interior = fine_sweep(lefts)
    cpoints = many(blocks[:, COARSEN - 1], interior[-1], 0.25)
    lefts = shifted(cpoints)
    interior = fine_sweep(lefts)
    resid = many(blocks[:, COARSEN - 1], interior[-1], 0.25) - cpoints
    restricted = cpoints
    rhs = restricted - many(firsts, lefts, 1.0) + resid

    def relax(values, phases):
        for phase in phases:
            update = many(firsts, shifted(values), 1.0) + rhs
            values = jnp.where(position == phase, update, values)
        return values

    phases = list(range(COARSEN - 1))
    coarse = relax(restricted, phases + [COARSEN - 1] + phases)
    second = rhs - (coarse - many(firsts, shifted(coarse), 1.0))
    owners = slice(COARSEN - 1, None, COARSEN)
    upper = coarse[owners]
    upper_w = firsts[owners]
    upper_prev = jnp.concatenate([inputs[None], upper[:-1]], 0)
    coarse_rhs = upper - many(upper_w, upper_prev, 4.0) + second[owners]
    solved = []
    current = inputs
    for index in range(points // COARSEN):
        current = advance(upper_w[index], current, 4.0) + coarse_rhs[index]
        solved.append(current)
    coarse = coarse.at[owners].add(jnp.stack(solved, 0) - upper)
    coarse = relax(coarse, phases)
    cpoints = cpoints + coarse - restricted
    interior = fine_sweep(shifted(cpoints))
    states = jnp.stack(interior + [cpoints], 1)
    return states.reshape(points * COARSEN, weights.shape[1], inputs.shape[1])
```

```python
import functools

import jax
import jax.numpy as jnp
from jax import lax
from jax.experimental import pallas as pl
from jax.experimental.pallas import tpu as pltpu
from jax.sharding import PartitionSpec as P

SIDE = 16
CELLS = 256
CHANS = 256
TAPS = 9 * CHANS
COARSEN = 4
DEVICES = 16
F32 = jnp.float32
BF16 = jnp.bfloat16
STATE = (CELLS, CHANS)
VMEM_LIMIT = 28 << 20


def conv_tanh(state, weight):
    column = lax.broadcasted_iota(jnp.int32, STATE, 0) % SIDE
    before = jnp.where(column == 0, 0.0, pltpu.roll(state, 1, 0)).astype(BF16)
    after = jnp.where(column == SIDE - 1, 0.0, pltpu.roll(state, CELLS - 1, 0)).astype(BF16)
    trio = [before, state.astype(BF16), after]
    edge = jnp.zeros((SIDE, CHANS), BF16)
    above = [jnp.concatenate([edge, x[:-SIDE]], 0) for x in trio]
    below = [jnp.concatenate([x[SIDE:], edge], 0) for x in trio]
    total = None
    for tap, piece in enumerate(above + trio + below):
        part = lax.dot_general(
            piece,
            weight[:, tap * CHANS : (tap + 1) * CHANS],
            (((1,), (1,)), ((), ())),
            preferred_element_type=F32,
        )
        total = part if total is None else total + part
    return jnp.tanh(total)


def vmem(shape, dtype):
    return pltpu.VMEM(shape, dtype)


def kernel_call(body, outs, args, name, steps, anywhere=(), scratch=()):
    args = [
        a if i in anywhere else pltpu.with_memory_space_constraint(a, pltpu.VMEM)
        for i, a in enumerate(args)
    ]
    return pl.pallas_call(
        body,
        out_shape=outs,
        in_specs=[
            pl.BlockSpec(memory_space=pl.ANY if i in anywhere else pltpu.VMEM)
            for i in range(len(args))
        ],
        out_specs=[pl.BlockSpec(memory_space=pltpu.VMEM) for _ in outs],
        scratch_shapes=list(scratch),
        compiler_params=pltpu.CompilerParams(vmem_limit_bytes=VMEM_LIMIT),
        cost_estimate=pl.CostEstimate(
            flops=steps * 2 * TAPS * CELLS * CHANS, bytes_accessed=1 << 20, transcendentals=0
        ),
        name=name,
    )(*args)


def place():
    return lax.axis_index("layer")


def first_sweep(inputs, guess, weights, cpoint, held, start, sems):
    copies = [
        pltpu.make_async_copy(weights.at[i], held.at[i], sems.at[i]) for i in range(COARSEN)
    ]
    for copy in copies:
        copy.start()
    start[...] = inputs[...].T
    state = jnp.where(place() == 0, inputs[...], guess[0]).T
    for i in range(COARSEN):
        copies[i].wait()
        state = state + 0.25 * conv_tanh(state, held[i])
    cpoint[...] = state.astype(BF16)


def second_sweep(left, start, held, rhs, pack):
    state = jnp.where(place() == 0, start[...], left[...].astype(F32))
    terms = []
    for i in range(COARSEN):
        terms.append(conv_tanh(state, held[i]))
        state = state + 0.25 * terms[-1]
    own = 0.25 * (terms[0] + terms[1] + terms[2] + terms[3]) - terms[0]
    rhs[...] = own
    pack[0] = state
    pack[1] = own


def stage1(pack, rhs, held, out):
    @pl.when(place() % 4 == 1)
    def _():
        first = pack[0]
        out[...] = (first + conv_tanh(first, held[0]) + rhs[...]).astype(BF16)


def both_steps(value, pack, rhs, even_w, held):
    value = value + conv_tanh(value, even_w[...]) + pack[1]
    return value + conv_tanh(value, held[0]) + rhs[...]


def stage2(got, pack, rhs, even_w, held, out, wide):
    @pl.when(place() % 4 == 3)
    def _():
        value = both_steps(got[...].astype(F32), pack, rhs, even_w, held)
        wide[...] = value
        out[...] = value.astype(BF16)


def stage3(got, upper, pack, rhs, even_w, held, out, xi):
    me = place()

    @pl.when((me % 4 == 1) & (me > 4))
    def _():
        out[...] = both_steps(got[...].astype(F32), pack, rhs, even_w, held).astype(BF16)

    @pl.when((me % 4 == 3) & (me > 4))
    def _():
        value = upper[...].astype(F32)
        xi[...] = value + 4.0 * conv_tanh(value, held[0])


def stage4(got, xi, pack, rhs, even_w, held, out, wide, second):
    me = place()

    @pl.when((me % 4 == 3) & (me > 4))
    def _():
        value = both_steps(got[...].astype(F32), pack, rhs, even_w, held)
        wide[...] = value
        out[...] = value.astype(BF16)
        second[...] = value - xi[...]


def stage56(owner, runner, got, carried, second, pack, rhs, even_w, held, out, wide):
    me = place()

    @pl.when(me == owner)
    def _():
        value = got[...].astype(F32)
        value = value + 4.0 * conv_tanh(value, held[0]) + second[...]
        wide[...] = value
        out[...] = value.astype(BF16)

    @pl.when(me == runner)
    def _():
        out[...] = both_steps(carried[...].astype(F32), pack, rhs, even_w, held).astype(BF16)


def last_sweep(last, final, start, solved1, solved2, solved3, solved4, pack, rhs, even_w, held, states, left):
    me = place()

    @pl.when(me == 0)
    def _():
        left[...] = start[...]

    @pl.when((me % 2 == 0) & (me > 0))
    def _():
        left[...] = jnp.where(me == 14, last[...], final[...]).astype(F32)

    @pl.when(me % 2 == 1)
    def _():
        value = jnp.where(me == 15, last[...], final[...]).astype(F32)
        value = jnp.where(me == 1, start[...], value)
        left[...] = value + conv_tanh(value, even_w[...]) + pack[1]

    state = left[...]
    term = conv_tanh(state, held[0])
    left[...] = state + term + rhs[...]
    for owner, solved in ((3, solved1), (7, solved2), (11, solved3), (15, solved4)):

        @pl.when(me == owner)
        def _():
            left[...] = solved[...]

    states[3] = left[...].T
    state = state + 0.25 * term
    states[0] = state.T
    for i in range(1, COARSEN - 1):
        state = state + 0.25 * conv_tanh(state, held[i])
        states[i] = state.T


def per_device(inputs, guess, weights):
    me = lax.axis_index("layer")

    def send(value, pairs):
        return lax.ppermute(value, "layer", pairs)

    narrow = vmem(STATE, BF16)
    wide = vmem(STATE, F32)
    intra_up = [(i, i + 1) for i in range(0, DEVICES, 2)]

    even_w = send(weights[0], intra_up)
    cpoint, held, start = kernel_call(
        first_sweep,
        [narrow, vmem((COARSEN, CHANS, TAPS), BF16), wide],
        [inputs, guess, weights],
        "first_sweep",
        4,
        anywhere=(2,),
        scratch=[pltpu.SemaphoreType.DMA((COARSEN,))],
    )
    left = send(cpoint, [(i, i + 1) for i in range(DEVICES - 1)])
    rhs, pack = kernel_call(
        second_sweep, [wide, vmem((2, *STATE), F32)], [left, start, held], "second_sweep", 4
    )
    pack = send(pack, intra_up)
    common = [pack, rhs, even_w, held]

    (c1,) = kernel_call(stage1, [narrow], [pack, rhs, held], "stage1", 1)
    got3 = send(c1, [(1, 3), (5, 7), (9, 11), (13, 15)])
    upper, wide1 = kernel_call(stage2, [narrow, wide], [got3, *common], "stage2", 2)
    got4 = send(upper, [(3, 5), (7, 9), (11, 13)])
    upper_prev = send(upper, [(3, 7), (7, 11), (11, 15)])
    c2, xi = kernel_call(stage3, [narrow, wide], [got4, upper_prev, *common], "stage3", 2)
    got5 = send(c2, [(5, 7), (9, 11), (13, 15)])
    z2, wide2, second = kernel_call(
        stage4, [narrow, wide, wide], [got5, xi, *common], "stage4", 2
    )
    got6 = send(z2, [(7, 11)])
    got6b = send(z2, [(7, 9)])
    z3, wide3 = kernel_call(
        functools.partial(stage56, 11, 9),
        [narrow, wide],
        [got6, got6b, second, *common],
        "stage5",
        2,
    )
    got7 = send(z3, [(11, 13), (9, 11)])
    got7b = send(z3, [(11, 15)])
    z4, wide4 = kernel_call(
        functools.partial(stage56, 15, 13),
        [narrow, wide],
        [got7b, got7, second, *common],
        "stage6",
        2,
    )
    got8 = send(z4, [(13, 15)])
    got8b = send(z4, [(13, 14)])
    final = got3
    for chip, got in ((2, got4), (3, got5), (4, got6b), (5, got7), (6, got7)):
        final = jnp.where(me == 2 * chip + 1, got, final)
    handed = send(final, [(2 * chip + 1, 2 * chip) for chip in range(1, 7)])
    final = jnp.where(me % 2 == 0, handed, final)
    last = jnp.where(me == 14, got8b, got8)
    return kernel_call(
        last_sweep,
        [jax.ShapeDtypeStruct((COARSEN, CHANS, CELLS), F32)],
        [last, final, start, wide1, wide2, wide3, wide4, *common],
        "last_sweep",
        4,
        scratch=[pltpu.VMEM(STATE, F32)],
    )[0]


def solution(mesh):
    return jax.shard_map(
        per_device,
        mesh=mesh,
        in_specs=(P(None, "batch"), P("layer", None, "batch"), P("layer", None, None)),
        out_specs=P("layer", None, "batch"),
        check_vma=False,
    )
```

```python
import functools

import jax
import jax.numpy as jnp
from jax import lax
from jax.experimental import pallas as pl
from jax.experimental.pallas import tpu as pltpu
from jax.sharding import PartitionSpec as P

SIDE = 16
CELLS = 256
CHANS = 256
TAPS = 9 * CHANS
COARSEN = 4
DEVICES = 16
F32 = jnp.float32
BF16 = jnp.bfloat16
STATE = (CELLS, CHANS)
VMEM_LIMIT = 12 << 20


def conv_tanh(state, weight):
    column = lax.broadcasted_iota(jnp.int32, STATE, 0) % SIDE
    before = jnp.where(column == 0, 0.0, pltpu.roll(state, 1, 0)).astype(BF16)
    after = jnp.where(column == SIDE - 1, 0.0, pltpu.roll(state, CELLS - 1, 0)).astype(BF16)
    trio = [before, state.astype(BF16), after]
    edge = jnp.zeros((SIDE, CHANS), BF16)
    above = [jnp.concatenate([edge, x[:-SIDE]], 0) for x in trio]
    below = [jnp.concatenate([x[SIDE:], edge], 0) for x in trio]
    total = None
    for tap, piece in enumerate(above + trio + below):
        part = lax.dot_general(
            piece,
            weight[:, tap * CHANS : (tap + 1) * CHANS],
            (((1,), (1,)), ((), ())),
            preferred_element_type=F32,
        )
        total = part if total is None else total + part
    return jnp.tanh(total)


def vmem(shape, dtype):
    return pltpu.VMEM(shape, dtype)


def kernel_call(body, outs, args, name, steps, hbm=(), scratch=(), aliases=None):
    def space(i):
        return pltpu.HBM if i in hbm else pltpu.VMEM

    args = [pltpu.with_memory_space_constraint(a, space(i)) for i, a in enumerate(args)]
    return pl.pallas_call(
        body,
        out_shape=outs,
        in_specs=[pl.BlockSpec(memory_space=space(i)) for i in range(len(args))],
        out_specs=[
            pl.BlockSpec(memory_space=pltpu.VMEM if hasattr(o, "memory_space") else pl.ANY)
            for o in outs
        ],
        scratch_shapes=list(scratch),
        input_output_aliases=aliases or {},
        compiler_params=pltpu.CompilerParams(vmem_limit_bytes=VMEM_LIMIT),
        cost_estimate=pl.CostEstimate(
            flops=steps * 2 * TAPS * CELLS * CHANS, bytes_accessed=1 << 20, transcendentals=0
        ),
        name=name,
    )(*args)


def place():
    return lax.axis_index("layer")


def first_sweep(parity, *refs):
    inputs, guess, weights = refs[:3]
    cpoint, own_w, later_w, start, raw, sems = refs[-6:]
    me = place()

    @pl.when(me % 2 == parity)
    def _():
        copies = [pltpu.make_async_copy(guess.at[0], raw.at[0], sems.at[0])]
        copies.append(pltpu.make_async_copy(inputs, raw.at[1], sems.at[1]))
        copies.append(pltpu.make_async_copy(weights.at[0], own_w, sems.at[2]))
        for i in range(COARSEN - 1):
            copies.append(
                pltpu.make_async_copy(weights.at[i + 1], later_w.at[i], sems.at[i + 3])
            )
        for copy in copies:
            copy.start()
        copies[0].wait()
        copies[1].wait()
        start[...] = raw[1].T
        state = jnp.where(me == 0, raw[1], raw[0]).T
        copies[2].wait()
        state = state + 0.25 * conv_tanh(state, own_w)
        for i in range(COARSEN - 1):
            copies[i + 3].wait()
            state = state + 0.25 * conv_tanh(state, later_w[i])
        cpoint[...] = state.astype(BF16)


def second_sweep(left_even, left_odd, start, own_w, later_w, rhs, first):
    me = place()
    left = jnp.where(me % 2 == 0, left_even[...], left_odd[...]).astype(F32)
    state = jnp.where(me == 0, start[...], left)
    terms = []
    for i in range(COARSEN):
        terms.append(conv_tanh(state, own_w if i == 0 else later_w[i - 1]))
        state = state + 0.25 * terms[-1]
    rhs[...] = 0.25 * (terms[0] + terms[1] + terms[2] + terms[3]) - terms[0]
    first[...] = state


def stage1(first, rhs, own_w, out):
    @pl.when(place() % 4 == 1)
    def _():
        value = first[...]
        out[...] = (value + conv_tanh(value, own_w) + rhs[...]).astype(BF16)


def both_steps(got, even_rhs, rhs, even_w, own_w):
    value = got[...].astype(F32)
    value = value + conv_tanh(value, even_w) + even_rhs[...]
    return value + conv_tanh(value, own_w) + rhs[...]


def stage2(got, even_rhs, rhs, even_w, own_w, out, solved):
    @pl.when(place() % 4 == 3)
    def _():
        value = both_steps(got, even_rhs, rhs, even_w, own_w)
        solved[...] = value
        out[...] = value.astype(BF16)


def stage3(got, even_rhs, rhs, even_w, own_w, out):
    me = place()

    @pl.when((me % 4 == 1) & (me > 4))
    def _():
        out[...] = both_steps(got, even_rhs, rhs, even_w, own_w).astype(BF16)


def stage4(got, upper, _, even_rhs, rhs, even_w, own_w, out, solved, passed):
    me = place()

    @pl.when((me % 4 == 3) & (me > 4))
    def _():
        value = both_steps(got, even_rhs, rhs, even_w, own_w)
        solved[...] = value
        out[...] = value.astype(BF16)

    @pl.when((me == 9) | (me == 13))
    def _():
        passed[...] = upper[...]


def coarse_rhs(upper, solved, own_w, out):
    me = place()

    @pl.when((me == 11) | (me == 15))
    def _():
        value = upper[...].astype(F32)
        out[...] = solved[...] - (value + 4.0 * conv_tanh(value, own_w))


def coarse_step(got, second, own_w):
    value = got[...].astype(F32)
    return value + 4.0 * conv_tanh(value, own_w) + second[...]


def stage5(got, second, early3, early4, mine, _, own_w, out, solved):
    me = place()

    @pl.when(me == 11)
    def _():
        value = coarse_step(got, second, own_w)
        solved[...] = value
        out[...] = value.astype(BF16)

    for owner, source in ((3, early3), (5, early4), (7, mine)):

        @pl.when(me == owner)
        def _():
            out[...] = source[...]


def stage6(got, mine, early5, even_rhs, rhs, even_w, own_w, out):
    me = place()

    @pl.when((me == 13) | (me == 9))
    def _():
        out[...] = both_steps(got, even_rhs, rhs, even_w, own_w).astype(BF16)

    for owner, source in ((11, mine), (7, early5)):

        @pl.when(me == owner)
        def _():
            out[...] = source[...]


def stage6_owner(got, second, _, own_w, solved):
    @pl.when(place() == 15)
    def _():
        solved[...] = coarse_step(got, second, own_w)


def last_sweep(
    start, got3, got4, got5, got7, got7b, got8, got8b, solved,
    even_rhs, rhs, even_w, own_w, later_w, states, left, ready, sems,
):
    me = place()
    sources = (
        (start, (0, 1)),
        (got7b, (2, 4, 8)),
        (got8b, (6, 10, 12, 14)),
        (got3, (3,)),
        (got4, (5,)),
        (got5, (7,)),
        (got7, (9, 13)),
        (got8, (11, 15)),
    )
    for source, owners in sources:
        chosen = me == owners[0]
        for owner in owners[1:]:
            chosen |= me == owner

        @pl.when(chosen)
        def _():
            left[...] = source[...].astype(F32)

    @pl.when(me % 2 == 1)
    def _():
        value = left[...]
        left[...] = value + conv_tanh(value, even_w) + even_rhs[...]

    def store(i, value):
        ready[i] = value.T
        copy = pltpu.make_async_copy(ready.at[i], states.at[i], sems.at[i])
        copy.start()
        return copy

    state = left[...]
    term = conv_tanh(state, own_w)
    end = jnp.where(me % 4 == 3, solved[...], state + term + rhs[...])
    copies = [store(COARSEN - 1, end)]
    state = state + 0.25 * term
    copies.append(store(0, state))
    for i in range(1, COARSEN - 1):
        state = state + 0.25 * conv_tanh(state, later_w[i - 1])
        copies.append(store(i, state))
    for copy in copies:
        copy.wait()


def per_device(inputs, guess, weights):
    def send(value, pairs):
        return lax.ppermute(value, "layer", pairs)

    narrow = vmem(STATE, BF16)
    wide = vmem(STATE, F32)
    held = [vmem((CHANS, TAPS), BF16), vmem((COARSEN - 1, CHANS, TAPS), BF16), wide]
    up_inside = [(i, i + 1) for i in range(0, DEVICES, 2)]
    up_between = [(i, i + 1) for i in range(1, DEVICES - 1, 2)]
    scratch = [pltpu.VMEM((2, CHANS, CELLS), F32), pltpu.SemaphoreType.DMA((COARSEN + 2,))]

    from_odd, *kept = kernel_call(
        functools.partial(first_sweep, 1),
        [narrow, *held],
        [inputs, guess, weights],
        "first_sweep_odd",
        4,
        hbm=(0, 1, 2),
        scratch=scratch,
    )
    left_even = send(from_odd, up_between)
    from_even, own_w, later_w, start = kernel_call(
        functools.partial(first_sweep, 0),
        [narrow, *held],
        [inputs, guess, weights, *kept],
        "first_sweep_even",
        4,
        hbm=(0, 1, 2),
        scratch=scratch,
        aliases={3: 1, 4: 2, 5: 3},
    )
    left_odd = send(from_even, up_inside)
    even_w = send(own_w, up_inside)
    rhs, first = kernel_call(
        second_sweep, [wide, wide], [left_even, left_odd, start, own_w, later_w], "second_sweep", 4
    )
    first = send(first, [(i, i + 1) for i in range(0, DEVICES, 4)])
    even_rhs = send(rhs, up_inside)
    common = [even_rhs, rhs, even_w, own_w]

    (c1,) = kernel_call(stage1, [narrow], [first, rhs, own_w], "stage1", 1)
    got3 = send(c1, [(1, 3), (5, 7), (9, 11), (13, 15)])
    upper, solved = kernel_call(stage2, [narrow, wide], [got3, *common], "stage2", 2)
    got4 = send(upper, [(3, 5), (7, 9), (11, 13)])
    (c2,) = kernel_call(stage3, [narrow], [got4, *common], "stage3", 2)
    got5 = send(c2, [(5, 7), (9, 11), (13, 15)])
    z2, solved, passed = kernel_call(
        stage4, [narrow, wide, narrow], [got5, got4, solved, *common], "stage4", 2, aliases={2: 1}
    )
    got6 = send(z2, [(7, 11)])
    upper_prev = send(passed, [(9, 11), (13, 15)])
    (second,) = kernel_call(coarse_rhs, [wide], [upper_prev, solved, own_w], "coarse_rhs", 1)
    z3, solved = kernel_call(
        stage5,
        [narrow, wide],
        [got6, second, got3, got4, z2, solved, own_w],
        "stage5",
        1,
        aliases={5: 1},
    )
    got7 = send(z3, [(11, 13), (7, 9)])
    got7b = send(z3, [(11, 15), (3, 2), (5, 4), (7, 8)])
    (c3,) = kernel_call(stage6, [narrow], [got7, z3, got5, *common], "stage6", 2)
    got8 = send(c3, [(13, 15), (9, 11)])
    got8b = send(c3, [(13, 14), (9, 10), (11, 12), (7, 6)])
    (solved,) = kernel_call(
        stage6_owner, [wide], [got7b, second, solved, own_w], "stage6_owner", 1, aliases={2: 0}
    )
    return kernel_call(
        last_sweep,
        [jax.ShapeDtypeStruct((COARSEN, CHANS, CELLS), F32)],
        [start, got3, got4, got5, got7, got7b, got8, got8b, solved, *common, later_w],
        "last_sweep",
        4,
        scratch=[
            pltpu.VMEM(STATE, F32),
            pltpu.VMEM((COARSEN, CHANS, CELLS), F32),
            pltpu.SemaphoreType.DMA((COARSEN,)),
        ],
    )[0]


def solution(mesh):
    return jax.shard_map(
        per_device,
        mesh=mesh,
        in_specs=(P(None, "batch"), P("layer", None, "batch"), P("layer", None, None)),
        out_specs=P("layer", None, "batch"),
        check_vma=False,
    )
```

```python
import functools

import jax
import jax.numpy as jnp
from jax import lax
from jax.experimental import pallas as pl
from jax.experimental.pallas import tpu as pltpu
from jax.sharding import PartitionSpec as P

SIDE = 16
CELLS = 256
CHANS = 256
TAPS = 9 * CHANS
COARSEN = 4
DEVICES = 16
F32 = jnp.float32
BF16 = jnp.bfloat16
STATE = (CELLS, CHANS)
VMEM_LIMIT = 12 << 20


def conv_tanh(state, weight):
    column = lax.broadcasted_iota(jnp.int32, STATE, 0) % SIDE
    before = jnp.where(column == 0, 0.0, pltpu.roll(state, 1, 0)).astype(BF16)
    after = jnp.where(column == SIDE - 1, 0.0, pltpu.roll(state, CELLS - 1, 0)).astype(BF16)
    trio = [before, state.astype(BF16), after]
    edge = jnp.zeros((SIDE, CHANS), BF16)
    above = [jnp.concatenate([edge, x[:-SIDE]], 0) for x in trio]
    below = [jnp.concatenate([x[SIDE:], edge], 0) for x in trio]
    total = None
    for tap, piece in enumerate(above + trio + below):
        part = lax.dot_general(
            piece,
            weight[:, tap * CHANS : (tap + 1) * CHANS],
            (((1,), (1,)), ((), ())),
            preferred_element_type=F32,
        )
        total = part if total is None else total + part
    return jnp.tanh(total)


def vmem(shape, dtype):
    return pltpu.VMEM(shape, dtype)


def kernel_call(body, outs, args, name, steps, hbm=(), scratch=(), aliases=None):
    def space(i):
        return pltpu.HBM if i in hbm else pltpu.VMEM

    args = [pltpu.with_memory_space_constraint(a, space(i)) for i, a in enumerate(args)]
    return pl.pallas_call(
        body,
        out_shape=outs,
        in_specs=[pl.BlockSpec(memory_space=space(i)) for i in range(len(args))],
        out_specs=[
            pl.BlockSpec(memory_space=pltpu.VMEM if hasattr(o, "memory_space") else pl.ANY)
            for o in outs
        ],
        scratch_shapes=list(scratch),
        input_output_aliases=aliases or {},
        compiler_params=pltpu.CompilerParams(vmem_limit_bytes=VMEM_LIMIT),
        cost_estimate=pl.CostEstimate(
            flops=steps * 2 * TAPS * CELLS * CHANS, bytes_accessed=1 << 20, transcendentals=0
        ),
        name=name,
    )(*args)


def place():
    return lax.axis_index("layer")


def first_sweep(parity, *refs):
    inputs, guess, weights = refs[:3]
    cpoint, own_w, later_w, start, raw, sems = refs[-6:]
    me = place()

    @pl.when(me % 2 == parity)
    def _():
        source = [pltpu.make_async_copy(weights.at[0], own_w, sems.at[1])]
        for i in range(COARSEN - 1):
            source.append(pltpu.make_async_copy(weights.at[i + 1], later_w.at[i], sems.at[i + 2]))
        begin = pltpu.make_async_copy(inputs, raw, sems.at[0])
        other = pltpu.make_async_copy(guess.at[0], raw, sems.at[0])

        @pl.when(me == 0)
        def _():
            begin.start()

        @pl.when(me > 0)
        def _():
            other.start()

        for copy in source:
            copy.start()
        other.wait()
        state = raw[...].T

        @pl.when(me == 0)
        def _():
            start[...] = state

        for i in range(COARSEN):
            source[i].wait()
            state = state + 0.25 * conv_tanh(state, own_w if i == 0 else later_w[i - 1])
        cpoint[...] = state.astype(BF16)

        @pl.when(me == 1)
        def _():
            begin.start()
            begin.wait()
            start[...] = raw[...].T


def sweep(state, own_w, later_w, rhs):
    terms = []
    for i in range(COARSEN):
        terms.append(conv_tanh(state, own_w if i == 0 else later_w[i - 1]))
        state = state + 0.25 * terms[-1]
    rhs[...] = 0.25 * (terms[0] + terms[1] + terms[2] + terms[3]) - terms[0]
    return state


def second_sweep_lead(left_odd, own_w, later_w, _, rhs, solved, out):
    @pl.when(place() == 1)
    def _():
        out[...] = sweep(left_odd[...].astype(F32), own_w, later_w, rhs).astype(BF16)


def second_sweep(left_odd, left_even, own_w, later_w, start, _, rhs, first):
    me = place()

    @pl.when(me != 1)
    def _():
        left = jnp.where(me % 2 == 0, left_even[...], left_odd[...]).astype(F32)
        first[...] = sweep(jnp.where(me == 0, start[...], left), own_w, later_w, rhs)


def in_order(*refs):
    pass


def either(me, owners):
    chosen = me == owners[0]
    for owner in owners[1:]:
        chosen |= me == owner
    return chosen


def two_steps(owners, keep, even_rhs, rhs, even_w, own_w, got, _, out, solved):
    @pl.when(either(place(), owners))
    def _():
        value = got[...].astype(F32)
        value = value + conv_tanh(value, even_w) + even_rhs[...]
        value = value + conv_tanh(value, own_w) + rhs[...]
        if keep:
            solved[...] = value
        out[...] = value.astype(BF16)


def one_step(owners, first, rhs, own_w, _, out, solved):
    @pl.when(either(place(), owners))
    def _():
        value = first[...]
        out[...] = (value + conv_tanh(value, own_w) + rhs[...]).astype(BF16)


def coarse_step(got, own_w):
    value = got[...].astype(F32)
    return value + 4.0 * conv_tanh(value, own_w)


def coarse_base(owners, upper, own_w, _, out, solved):
    @pl.when(either(place(), owners))
    def _():
        out[...] = coarse_step(upper, own_w)


def lead_step(got, base, own_w, early3, early4, mine, _, out, solved):
    me = place()

    @pl.when(me == 11)
    def _():
        value = coarse_step(got, own_w) + (solved[...] - base[...])
        solved[...] = value
        out[...] = value.astype(BF16)

    for owner, source in ((3, early3), (5, early4), (7, mine)):

        @pl.when(me == owner)
        def _():
            out[...] = source[...]


def lead_two_steps(got, mine, early5, even_rhs, rhs, even_w, own_w, _, out, solved):
    two_steps((9, 13), False, even_rhs, rhs, even_w, own_w, got, _, out, solved)
    for owner, source in ((11, mine), (7, early5)):

        @pl.when(place() == owner)
        def _():
            out[...] = source[...]


def end_step(got, base, own_w, _, solved):
    @pl.when(place() == 15)
    def _():
        solved[...] = coarse_step(got, own_w) + (solved[...] - base[...])


def last_sweep(
    start, got8b, got8, got3, got4, got5, got7, got7b,
    even_rhs, rhs, even_w, own_w, later_w, solved, states, left, ready, sems,
):
    me = place()
    sources = (
        (start, (0, 1)),
        (got7b, (2, 4, 8)),
        (got8b, (6, 10, 12, 14)),
        (got3, (3,)),
        (got4, (5,)),
        (got5, (7,)),
        (got7, (9, 13)),
        (got8, (11, 15)),
    )
    for source, owners in sources:

        @pl.when(either(me, owners))
        def _():
            left[...] = source[...].astype(F32)

    @pl.when(me % 2 == 1)
    def _():
        value = left[...]
        left[...] = value + conv_tanh(value, even_w) + even_rhs[...]

    def store(i, value):
        ready[i] = value.T
        copy = pltpu.make_async_copy(ready.at[i], states.at[i], sems.at[i])
        copy.start()
        return copy

    state = left[...]
    term = conv_tanh(state, own_w)
    end = jnp.where(me % 4 == 3, solved[...], state + term + rhs[...])
    copies = [store(COARSEN - 1, end)]
    state = state + 0.25 * term
    copies.append(store(0, state))
    for i in range(1, COARSEN - 1):
        state = state + 0.25 * conv_tanh(state, later_w[i - 1])
        copies.append(store(i, state))
    for copy in copies:
        copy.wait()


def per_device(inputs, guess, weights):
    def send(value, pairs):
        return lax.ppermute(value, "layer", pairs)

    narrow = vmem(STATE, BF16)
    wide = vmem(STATE, F32)
    held = [vmem((CHANS, TAPS), BF16), vmem((COARSEN - 1, CHANS, TAPS), BF16), wide]
    up_inside = [(i, i + 1) for i in range(0, DEVICES, 2)]
    up_between = [(i, i + 1) for i in range(1, DEVICES - 1, 2)]
    scratch = [pltpu.VMEM((CHANS, CELLS), F32), pltpu.SemaphoreType.DMA((COARSEN + 1,))]

    from_odd, *kept = kernel_call(
        functools.partial(first_sweep, 1),
        [narrow, *held],
        [inputs, guess, weights],
        "first_sweep_odd",
        4,
        hbm=(0, 1, 2),
        scratch=scratch,
    )
    left_even = send(from_odd, up_between)
    from_even, own_w, later_w, start = kernel_call(
        functools.partial(first_sweep, 0),
        [narrow, *held],
        [inputs, guess, weights, *kept],
        "first_sweep_even",
        4,
        hbm=(0, 1, 2),
        scratch=scratch,
        aliases={3: 1, 4: 2, 5: 3},
    )
    left_odd = send(from_even, up_inside)
    even_w = send(own_w, up_inside)

    left_even, start = kernel_call(
        in_order, [narrow, wide], [left_even, start], "even_first", 1, aliases={0: 0, 1: 1}
    )
    rhs, solved, c1 = kernel_call(
        second_sweep_lead,
        [wide, wide, narrow],
        [left_odd, own_w, later_w, start],
        "second_sweep_lead",
        40,
    )
    got3 = send(c1, [(1, 3)])
    rhs, first = kernel_call(
        second_sweep,
        [wide, wide],
        [left_odd, left_even, own_w, later_w, start, rhs],
        "second_sweep",
        4,
        aliases={5: 0},
    )
    first = send(first, [(4, 5), (8, 9)])
    even_rhs = send(rhs, up_inside)
    both = [even_rhs, rhs, even_w, own_w]
    got3, solved = kernel_call(
        in_order, [narrow, wide], [got3, solved], "lead_first", 10, aliases={0: 0, 1: 1}
    )

    def chained(body, args, name, steps, out=narrow):
        nonlocal solved
        value, solved = kernel_call(
            body, [out, wide], [*args, solved], name, steps, aliases={len(args): 1}
        )
        return value

    def pair(owners, keep, got, name):
        return chained(functools.partial(two_steps, owners, keep), [*both, got], name, 2)

    upper1 = pair((3,), True, got3, "relax_lead")
    got4 = send(upper1, [(3, 5)])
    c5 = chained(functools.partial(one_step, (5, 9)), [first, rhs, own_w], "relax_first", 1)
    got3_rest = send(c5, [(5, 7), (9, 11)])
    c5_lead = pair((5,), False, got4, "again_lead")
    got5 = send(c5_lead, [(5, 7)])
    upper = pair((7, 11), False, got3_rest, "relax_rest")
    got4_rest = send(upper, [(7, 9), (11, 13)])
    upper_prev = send(upper, [(7, 11), (11, 15)])
    z2 = pair((7,), True, got5, "again_end_lead")
    got6 = send(z2, [(7, 11)])
    c9 = pair((9, 13), False, got4_rest, "again_rest")
    got5_rest = send(c9, [(9, 11), (13, 15)])
    base = chained(
        functools.partial(coarse_base, (11, 15)), [upper_prev, own_w], "coarse_base", 1, wide
    )
    pair((11, 15), True, got5_rest, "again_end_rest")
    z3 = chained(lead_step, [got6, base, own_w, got3, got4, z2], "coarse_lead", 1)
    got7 = send(z3, [(11, 13), (7, 9)])
    got7b = send(z3, [(11, 15), (3, 2), (5, 4), (7, 8)])
    c13 = chained(lead_two_steps, [got7, z3, got5, *both], "final_lead", 2)
    got8 = send(c13, [(13, 15), (9, 11)])
    got8b = send(c13, [(13, 14), (9, 10), (11, 12), (7, 6)])
    (solved,) = kernel_call(
        end_step, [wide], [got7b, base, own_w, solved], "coarse_end", 1, aliases={3: 0}
    )
    return kernel_call(
        last_sweep,
        [jax.ShapeDtypeStruct((COARSEN, CHANS, CELLS), F32)],
        [start, got8b, got8, got3, got4, got5, got7, got7b, *both, later_w, solved],
        "last_sweep",
        4,
        scratch=[
            pltpu.VMEM(STATE, F32),
            pltpu.VMEM((COARSEN, CHANS, CELLS), F32),
            pltpu.SemaphoreType.DMA((COARSEN,)),
        ],
    )[0]


def solution(mesh):
    return jax.shard_map(
        per_device,
        mesh=mesh,
        in_specs=(P(None, "batch"), P("layer", None, "batch"), P("layer", None, None)),
        out_specs=P("layer", None, "batch"),
        check_vma=False,
    )
```

```python
import functools

import jax
import jax.numpy as jnp
from jax import lax
from jax.experimental import pallas as pl
from jax.experimental.pallas import tpu as pltpu
from jax.sharding import PartitionSpec as P

SIDE = 16
CELLS = 256
CHANS = 256
TAPS = 9 * CHANS
COARSEN = 4
DEVICES = 16
F32 = jnp.float32
BF16 = jnp.bfloat16
STATE = (CELLS, CHANS)
VMEM_LIMIT = 12 << 20


def conv_tanh(state, weight):
    column = lax.broadcasted_iota(jnp.int32, STATE, 0) % SIDE
    before = jnp.where(column == 0, 0.0, pltpu.roll(state, 1, 0)).astype(BF16)
    after = jnp.where(column == SIDE - 1, 0.0, pltpu.roll(state, CELLS - 1, 0)).astype(BF16)
    here = state.astype(BF16)
    edge = jnp.zeros((SIDE, CHANS), BF16)

    def product(piece, row, column):
        if row == 0:
            piece = jnp.concatenate([edge, piece[:-SIDE]], 0)
        if row == 2:
            piece = jnp.concatenate([piece[SIDE:], edge], 0)
        tap = 3 * row + column
        return lax.dot_general(
            piece,
            weight[:, tap * CHANS : (tap + 1) * CHANS],
            (((1,), (1,)), ((), ())),
            preferred_element_type=F32,
        )

    total = product(here, 1, 1)
    for column, piece in ((1, -here), (0, -before), (2, -after)):
        for row in (0, 2) if column == 1 else (1, 0, 2):
            total = total - product(piece, row, column)
    return jnp.tanh(total)


def vmem(shape, dtype):
    return pltpu.VMEM(shape, dtype)


def kernel_call(body, outs, args, name, steps, hbm=(), scratch=(), aliases=None):
    def space(i):
        return pltpu.HBM if i in hbm else pltpu.VMEM

    args = [pltpu.with_memory_space_constraint(a, space(i)) for i, a in enumerate(args)]
    return pl.pallas_call(
        body,
        out_shape=outs,
        in_specs=[pl.BlockSpec(memory_space=space(i)) for i in range(len(args))],
        out_specs=[
            pl.BlockSpec(memory_space=pltpu.VMEM if hasattr(o, "memory_space") else pl.ANY)
            for o in outs
        ],
        scratch_shapes=list(scratch),
        input_output_aliases=aliases or {},
        compiler_params=pltpu.CompilerParams(vmem_limit_bytes=VMEM_LIMIT),
        cost_estimate=pl.CostEstimate(
            flops=steps * 2 * TAPS * CELLS * CHANS, bytes_accessed=1 << 20, transcendentals=0
        ),
        name=name,
    )(*args)


def place():
    return lax.axis_index("layer")


def first_sweep(parity, *refs):
    inputs, guess, weights = refs[:3]
    cpoint, own_w, later_w, start, raw, sems = refs[-6:]
    me = place()

    @pl.when(me % 2 == parity)
    def _():
        source = [pltpu.make_async_copy(weights.at[0], own_w, sems.at[1])]
        for i in range(COARSEN - 1):
            source.append(pltpu.make_async_copy(weights.at[i + 1], later_w.at[i], sems.at[i + 2]))
        begin = pltpu.make_async_copy(inputs, raw, sems.at[0])
        other = pltpu.make_async_copy(guess.at[0], raw, sems.at[0])

        @pl.when(me == 0)
        def _():
            begin.start()

        @pl.when(me > 0)
        def _():
            other.start()

        for copy in source:
            copy.start()
        other.wait()
        state = raw[...].T

        @pl.when(me == 0)
        def _():
            start[...] = state

        for i in range(COARSEN):
            source[i].wait()
            state = state + 0.25 * conv_tanh(state, own_w if i == 0 else later_w[i - 1])
        cpoint[...] = state.astype(BF16)

        @pl.when(me == 1)
        def _():
            begin.start()
            begin.wait()
            start[...] = raw[...].T


def sweep(state, own_w, later_w, rhs):
    terms = []
    for i in range(COARSEN):
        terms.append(conv_tanh(state, own_w if i == 0 else later_w[i - 1]))
        state = state + 0.25 * terms[-1]
    rhs[...] = 0.25 * (terms[0] + terms[1] + terms[2] + terms[3]) - terms[0]
    return state


def second_sweep_lead(left_odd, own_w, later_w, _, rhs, solved, out):
    @pl.when(place() == 1)
    def _():
        out[...] = sweep(left_odd[...].astype(F32), own_w, later_w, rhs).astype(BF16)


def second_sweep(left_odd, left_even, own_w, later_w, start, _, rhs, first):
    me = place()

    @pl.when(me != 1)
    def _():
        left = jnp.where(me % 2 == 0, left_even[...], left_odd[...]).astype(F32)
        first[...] = sweep(jnp.where(me == 0, start[...], left), own_w, later_w, rhs)


def in_order(*refs):
    pass


def either(me, owners):
    chosen = me == owners[0]
    for owner in owners[1:]:
        chosen |= me == owner
    return chosen


def both_steps(even_rhs, rhs, even_w, own_w, got):
    value = got[...].astype(F32)
    value = value + conv_tanh(value, even_w) + even_rhs[...]
    return value + conv_tanh(value, own_w) + rhs[...]


def two_steps(owners, keep, even_rhs, rhs, even_w, own_w, got, _, out, solved):
    @pl.when(either(place(), owners))
    def _():
        value = both_steps(even_rhs, rhs, even_w, own_w, got)
        if keep:
            solved[...] = value
        out[...] = value.astype(BF16)


def lead_half(got, even_w, _, out, solved):
    @pl.when(place() == 3)
    def _():
        value = got[...].astype(F32)
        out[...] = value + conv_tanh(value, even_w)


def lead_rest(rhs, own_w, even_rhs, part, _, out, solved):
    @pl.when(place() == 3)
    def _():
        value = part[...] + even_rhs[...]
        value = value + conv_tanh(value, own_w) + rhs[...]
        solved[...] = value
        out[...] = value.astype(BF16)


def one_step(owners, first, rhs, own_w, _, out, solved):
    @pl.when(either(place(), owners))
    def _():
        value = first[...]
        out[...] = (value + conv_tanh(value, own_w) + rhs[...]).astype(BF16)


def coarse_step(got, own_w):
    value = got[...].astype(F32)
    return value + 4.0 * conv_tanh(value, own_w)


def steps_or_copy(owner, keep, upper, even_rhs, rhs, even_w, own_w, got, _, out, solved):
    two_steps((owner,), keep, even_rhs, rhs, even_w, own_w, got, _, out, solved)

    @pl.when(place() == 11)
    def _():
        out[...] = upper[...]


def coarse_base(upper, own_w, _, out, solved):
    @pl.when(place() == 11)
    def _():
        out[...] = coarse_step(upper, own_w)


def again_end(even_rhs, rhs, even_w, own_w, got, _, out, solved):
    @pl.when(either(place(), (11, 13)))
    def _():
        value = both_steps(even_rhs, rhs, even_w, own_w, got)
        solved[...] = value
        out[...] = value.astype(BF16)


def lead_step(got, base, own_w, early3, early4, mine, behind, _, out, solved):
    me = place()

    @pl.when(me == 11)
    def _():
        value = coarse_step(got, own_w) + (solved[...] - base[...])
        solved[...] = value
        out[...] = value.astype(BF16)

    for owner, source in ((3, early3), (5, early4), (7, mine), (13, behind)):

        @pl.when(me == owner)
        def _():
            out[...] = source[...]


def lead_two_steps(got, mine, early5, even_rhs, rhs, even_w, own_w, _, out, solved):
    two_steps((9, 13), False, even_rhs, rhs, even_w, own_w, got, _, out, solved)
    for owner, source in ((11, mine), (7, early5)):

        @pl.when(place() == owner)
        def _():
            out[...] = source[...]


def end_step(upper, even_rhs, rhs, even_w, own_w, got, lead, _, solved):
    @pl.when(place() == 15)
    def _():
        value = both_steps(even_rhs, rhs, even_w, own_w, got) - coarse_step(upper, own_w)
        solved[...] = value + coarse_step(lead, own_w)


def last_sweep(
    start, got8b, got8, got3, got4, got5, got7, got7b,
    even_rhs, rhs, even_w, own_w, later_w, solved, states, left, ready, sems,
):
    me = place()
    sources = (
        (start, (0, 1)),
        (got7b, (2, 4, 8)),
        (got8b, (6, 10, 12, 14)),
        (got3, (3,)),
        (got4, (5,)),
        (got5, (7,)),
        (got7, (9, 13)),
        (got8, (11, 15)),
    )
    for source, owners in sources:

        @pl.when(either(me, owners))
        def _():
            left[...] = source[...].astype(F32)

    @pl.when(me % 2 == 1)
    def _():
        value = left[...]
        left[...] = value + conv_tanh(value, even_w) + even_rhs[...]

    def store(i, value):
        ready[i] = value.T
        copy = pltpu.make_async_copy(ready.at[i], states.at[i], sems.at[i])
        copy.start()
        return copy

    state = left[...]
    term = conv_tanh(state, own_w)
    end = jnp.where(me % 4 == 3, solved[...], state + term + rhs[...])
    copies = [store(COARSEN - 1, end)]
    state = state + 0.25 * term
    copies.append(store(0, state))
    for i in range(1, COARSEN - 1):
        state = state + 0.25 * conv_tanh(state, later_w[i - 1])
        copies.append(store(i, state))
    for copy in copies:
        copy.wait()


def per_device(inputs, guess, weights):
    def send(value, pairs):
        return lax.ppermute(value, "layer", pairs)

    narrow = vmem(STATE, BF16)
    wide = vmem(STATE, F32)
    held = [vmem((CHANS, TAPS), BF16), vmem((COARSEN - 1, CHANS, TAPS), BF16), wide]
    up_inside = [(i, i + 1) for i in range(0, DEVICES, 2)]
    up_between = [(i, i + 1) for i in range(1, DEVICES - 1, 2)]
    scratch = [pltpu.VMEM((CHANS, CELLS), F32), pltpu.SemaphoreType.DMA((COARSEN + 1,))]

    from_odd, *kept = kernel_call(
        functools.partial(first_sweep, 1),
        [narrow, *held],
        [inputs, guess, weights],
        "first_sweep_odd",
        4,
        hbm=(0, 1, 2),
        scratch=scratch,
    )
    left_even = send(from_odd, up_between)
    from_even, own_w, later_w, start = kernel_call(
        functools.partial(first_sweep, 0),
        [narrow, *held],
        [inputs, guess, weights, *kept],
        "first_sweep_even",
        4,
        hbm=(0, 1, 2),
        scratch=scratch,
        aliases={3: 1, 4: 2, 5: 3},
    )
    left_odd = send(from_even, up_inside)
    even_w = send(own_w, up_inside)

    left_even, start = kernel_call(
        in_order, [narrow, wide], [left_even, start], "even_first", 1, aliases={0: 0, 1: 1}
    )
    rhs, solved, c1 = kernel_call(
        second_sweep_lead,
        [wide, wide, narrow],
        [left_odd, own_w, later_w, start],
        "second_sweep_lead",
        40,
    )
    got3 = send(c1, [(1, 3)])
    rhs, first = kernel_call(
        second_sweep,
        [wide, wide],
        [left_odd, left_even, own_w, later_w, start, rhs],
        "second_sweep",
        4,
        aliases={5: 0},
    )
    first = send(first, [(4, 5), (8, 9)])
    even_rhs = send(rhs, up_inside)
    both = [even_rhs, rhs, even_w, own_w]

    def chained(body, args, name, steps, out=narrow):
        nonlocal solved
        value, solved = kernel_call(
            body, [out, wide], [*args, solved], name, steps, aliases={len(args): 1}
        )
        return value

    def pair(owners, keep, got, name):
        return chained(functools.partial(two_steps, owners, keep), [*both, got], name, 2)

    part = chained(lead_half, [got3, even_w], "lead_first", 10, wide)
    upper1 = chained(lead_rest, [rhs, own_w, even_rhs, part], "relax_lead", 1)
    got4 = send(upper1, [(3, 5)])
    c5 = chained(functools.partial(one_step, (5, 9)), [first, rhs, own_w], "relax_first", 1)
    got3_rest = send(c5, [(5, 7), (9, 11)])
    c5_lead = pair((5,), False, got4, "again_lead")
    got5 = send(c5_lead, [(5, 7)])
    upper7 = pair((7,), False, got3_rest, "relax_rest")
    got4_rest = send(upper7, [(7, 9)])
    upper_prev = send(upper7, [(7, 11)])
    upper11 = pair((11,), False, got3_rest, "relax_last")
    z2 = chained(
        functools.partial(steps_or_copy, 7, True), [upper11, *both, got5], "again_end_lead", 2
    )
    got6 = send(z2, [(7, 11), (11, 15)])
    c9 = chained(
        functools.partial(steps_or_copy, 9, False), [upper11, *both, got4_rest], "again_rest", 2
    )
    got5_rest = send(c9, [(9, 11), (11, 13)])
    base = chained(coarse_base, [upper_prev, own_w], "coarse_base", 1, wide)
    c13 = chained(again_end, [*both, got5_rest], "again_end_rest", 2)
    z3 = chained(lead_step, [got6, base, own_w, got3, got4, z2, c13], "coarse_lead", 1)
    got7 = send(z3, [(11, 13), (7, 9), (13, 15)])
    got7b = send(z3, [(11, 15), (3, 2), (5, 4), (7, 8)])
    c13 = chained(lead_two_steps, [got7, z3, got5, *both], "final_lead", 2)
    got8 = send(c13, [(13, 15), (9, 11)])
    got8b = send(c13, [(13, 14), (9, 10), (11, 12), (7, 6)])
    (solved,) = kernel_call(
        end_step, [wide], [got6, *both, got7, got7b, solved], "coarse_end", 4, aliases={7: 0}
    )
    return kernel_call(
        last_sweep,
        [jax.ShapeDtypeStruct((COARSEN, CHANS, CELLS), F32)],
        [start, got8b, got8, got3, got4, got5, got7, got7b, *both, later_w, solved],
        "last_sweep",
        4,
        scratch=[
            pltpu.VMEM(STATE, F32),
            pltpu.VMEM((COARSEN, CHANS, CELLS), F32),
            pltpu.SemaphoreType.DMA((COARSEN,)),
        ],
    )[0]


def solution(mesh):
    return jax.shard_map(
        per_device,
        mesh=mesh,
        in_specs=(P(None, "batch"), P("layer", None, "batch"), P("layer", None, None)),
        out_specs=P("layer", None, "batch"),
        check_vma=False,
    )
```

```python
import functools

import jax
import jax.numpy as jnp
from jax import lax
from jax.experimental import pallas as pl
from jax.experimental.pallas import tpu as pltpu
from jax.sharding import PartitionSpec as P

SIDE = 16
CELLS = 256
CHANS = 256
TAPS = 9 * CHANS
COARSEN = 4
DEVICES = 16
F32 = jnp.float32
BF16 = jnp.bfloat16
STATE = (CELLS, CHANS)
VMEM_LIMIT = 12 << 20


def conv_tanh(state, weight):
    column = lax.broadcasted_iota(jnp.int32, STATE, 0) % SIDE
    before = jnp.where(column == 0, 0.0, pltpu.roll(state, 1, 0)).astype(BF16)
    after = jnp.where(column == SIDE - 1, 0.0, pltpu.roll(state, CELLS - 1, 0)).astype(BF16)
    here = state.astype(BF16)
    edge = jnp.zeros((SIDE, CHANS), BF16)

    def product(piece, row, column):
        if row == 0:
            piece = jnp.concatenate([edge, piece[:-SIDE]], 0)
        if row == 2:
            piece = jnp.concatenate([piece[SIDE:], edge], 0)
        tap = 3 * row + column
        return lax.dot_general(
            piece,
            weight[:, tap * CHANS : (tap + 1) * CHANS],
            (((1,), (1,)), ((), ())),
            preferred_element_type=F32,
        )

    total = product(here, 1, 1)
    for column, piece in ((1, -here), (0, -before), (2, -after)):
        for row in (0, 2) if column == 1 else (1, 0, 2):
            total = total - product(piece, row, column)
    return jnp.tanh(total)


def vmem(shape, dtype):
    return pltpu.VMEM(shape, dtype)


def kernel_call(body, outs, args, name, steps, hbm=(), scratch=(), aliases=None):
    def space(i):
        return pltpu.HBM if i in hbm else pltpu.VMEM

    args = [pltpu.with_memory_space_constraint(a, space(i)) for i, a in enumerate(args)]
    return pl.pallas_call(
        body,
        out_shape=outs,
        in_specs=[pl.BlockSpec(memory_space=space(i)) for i in range(len(args))],
        out_specs=[
            pl.BlockSpec(memory_space=pltpu.VMEM if hasattr(o, "memory_space") else pl.ANY)
            for o in outs
        ],
        scratch_shapes=list(scratch),
        input_output_aliases=aliases or {},
        compiler_params=pltpu.CompilerParams(vmem_limit_bytes=VMEM_LIMIT),
        cost_estimate=pl.CostEstimate(
            flops=steps * 2 * TAPS * CELLS * CHANS, bytes_accessed=1 << 20, transcendentals=0
        ),
        name=name,
    )(*args)


def place():
    return lax.axis_index("layer")


def first_sweep(first, *refs):
    inputs, guess, weights = refs[:3]
    cpoint, own_w, later_w, start, raw, sems = refs[-6:]
    me = place()

    early = (me % 2 == 1) | (me == 0)

    @pl.when(early if first else jnp.logical_not(early))
    def _():
        source = [pltpu.make_async_copy(weights.at[0], own_w, sems.at[1])]
        for i in range(COARSEN - 1):
            source.append(pltpu.make_async_copy(weights.at[i + 1], later_w.at[i], sems.at[i + 2]))
        begin = pltpu.make_async_copy(inputs, raw, sems.at[0])
        other = pltpu.make_async_copy(guess.at[0], raw, sems.at[0])

        @pl.when(me == 0)
        def _():
            begin.start()

        @pl.when(me > 0)
        def _():
            other.start()

        for copy in source:
            copy.start()
        other.wait()
        state = raw[...].T

        @pl.when(me == 0)
        def _():
            start[...] = state

        for i in range(COARSEN):
            source[i].wait()
            state = state + 0.25 * conv_tanh(state, own_w if i == 0 else later_w[i - 1])
        cpoint[...] = state.astype(BF16)

    if not first:

        @pl.when(me == 0)
        def _():
            cpoint[...] = refs[6][...]


def sweep(state, own_w, later_w, rhs):
    terms = []
    for i in range(COARSEN):
        terms.append(conv_tanh(state, own_w if i == 0 else later_w[i - 1]))
        state = state + 0.25 * terms[-1]
    rhs[...] = 0.25 * (terms[0] + terms[1] + terms[2] + terms[3]) - terms[0]
    return state


def second_sweep_lead(left_odd, own_w, later_w, _, rhs, solved, out):
    @pl.when(place() == 1)
    def _():
        out[...] = sweep(left_odd[...].astype(F32), own_w, later_w, rhs).astype(BF16)


def second_sweep_even(left_even, own_w, later_w, inputs, _, __, rhs, first, start, solved, raw, sem):
    me = place()

    @pl.when(me % 2 == 0)
    def _():
        left = jnp.where(me == 0, start[...], left_even[...].astype(F32))
        first[...] = sweep(left, own_w, later_w, rhs)

    @pl.when(me == 1)
    def _():
        copy = pltpu.make_async_copy(inputs, raw, sem)
        copy.start()
        copy.wait()
        start[...] = raw[...].T


def second_sweep_odd(left_odd, own_w, later_w, _, __, rhs, solved):
    me = place()

    @pl.when((me % 2 == 1) & (me > 1))
    def _():
        sweep(left_odd[...].astype(F32), own_w, later_w, rhs)


def in_order(*refs):
    pass


def either(me, owners):
    chosen = me == owners[0]
    for owner in owners[1:]:
        chosen |= me == owner
    return chosen


def both_steps(even_rhs, rhs, even_w, own_w, got):
    value = got[...].astype(F32)
    value = value + conv_tanh(value, even_w) + even_rhs[...]
    return value + conv_tanh(value, own_w) + rhs[...]


def two_steps(owners, keep, even_rhs, rhs, even_w, own_w, got, _, out, solved):
    @pl.when(either(place(), owners))
    def _():
        value = both_steps(even_rhs, rhs, even_w, own_w, got)
        if keep:
            solved[...] = value
        out[...] = value.astype(BF16)


def lead_half(got, even_w, _, out, solved):
    @pl.when(place() == 3)
    def _():
        value = got[...].astype(F32)
        out[...] = value + conv_tanh(value, even_w)


def lead_rest(rhs, own_w, even_rhs, part, _, out, solved):
    @pl.when(place() == 3)
    def _():
        value = part[...] + even_rhs[...]
        value = value + conv_tanh(value, own_w) + rhs[...]
        solved[...] = value
        out[...] = value.astype(BF16)


def one_step(owners, first, rhs, own_w, _, out, solved):
    @pl.when(either(place(), owners))
    def _():
        value = first[...]
        out[...] = (value + conv_tanh(value, own_w) + rhs[...]).astype(BF16)


def coarse_step(got, own_w):
    value = got[...].astype(F32)
    return value + 4.0 * conv_tanh(value, own_w)


def steps_or_copy(owner, keep, upper, even_rhs, rhs, even_w, own_w, got, _, out, solved):
    two_steps((owner,), keep, even_rhs, rhs, even_w, own_w, got, _, out, solved)

    @pl.when(place() == 11)
    def _():
        out[...] = upper[...]


def coarse_base(upper, own_w, _, out, solved):
    @pl.when(place() == 11)
    def _():
        out[...] = coarse_step(upper, own_w)


def again_end(even_rhs, rhs, even_w, own_w, got, _, out, solved):
    @pl.when(either(place(), (11, 13)))
    def _():
        value = both_steps(even_rhs, rhs, even_w, own_w, got)
        solved[...] = value
        out[...] = value.astype(BF16)


def lead_step(got, base, own_w, early3, early4, mine, behind, _, out, solved):
    me = place()

    @pl.when(me == 11)
    def _():
        value = coarse_step(got, own_w) + (solved[...] - base[...])
        solved[...] = value
        out[...] = value.astype(BF16)

    for owner, source in ((3, early3), (5, early4), (7, mine), (13, behind)):

        @pl.when(me == owner)
        def _():
            out[...] = source[...]


def lead_two_steps(got, mine, early5, even_rhs, rhs, even_w, own_w, _, out, solved):
    two_steps((9, 13), False, even_rhs, rhs, even_w, own_w, got, _, out, solved)
    for owner, source in ((11, mine), (7, early5)):

        @pl.when(place() == owner)
        def _():
            out[...] = source[...]


def end_step(upper, even_rhs, rhs, even_w, own_w, got, lead, _, solved):
    @pl.when(place() == 15)
    def _():
        value = both_steps(even_rhs, rhs, even_w, own_w, got) - coarse_step(upper, own_w)
        solved[...] = value + coarse_step(lead, own_w)


def last_sweep(
    start, got8b, got8, got3, got4, got5, got7, got7b,
    even_rhs, rhs, even_w, own_w, rhs_of_even, later_w, solved, states, left, ready, sems,
):
    me = place()
    sources = (
        (start, (0, 1)),
        (got7b, (2, 4, 8)),
        (got8b, (6, 10, 12, 14)),
        (got3, (3,)),
        (got4, (5,)),
        (got5, (7,)),
        (got7, (9, 13)),
        (got8, (11, 15)),
    )
    for source, owners in sources:

        @pl.when(either(me, owners))
        def _():
            left[...] = source[...].astype(F32)

    @pl.when(me % 2 == 1)
    def _():
        value = left[...]
        left[...] = value + conv_tanh(value, even_w) + even_rhs[...]

    def store(i, value):
        ready[i] = value.T
        copy = pltpu.make_async_copy(ready.at[i], states.at[i], sems.at[i])
        copy.start()
        return copy

    state = left[...]
    term = conv_tanh(state, own_w)
    own = jnp.where(me % 2 == 0, rhs_of_even[...], rhs[...])
    end = jnp.where(me % 4 == 3, solved[...], state + term + own)
    copies = [store(COARSEN - 1, end)]
    state = state + 0.25 * term
    copies.append(store(0, state))
    for i in range(1, COARSEN - 1):
        state = state + 0.25 * conv_tanh(state, later_w[i - 1])
        copies.append(store(i, state))
    for copy in copies:
        copy.wait()


def per_device(inputs, guess, weights):
    def send(value, pairs):
        return lax.ppermute(value, "layer", pairs)

    narrow = vmem(STATE, BF16)
    wide = vmem(STATE, F32)
    held = [vmem((CHANS, TAPS), BF16), vmem((COARSEN - 1, CHANS, TAPS), BF16), wide]
    up_inside = [(i, i + 1) for i in range(0, DEVICES, 2)]
    up_between = [(i, i + 1) for i in range(1, DEVICES - 1, 2)]
    scratch = [pltpu.VMEM((CHANS, CELLS), F32), pltpu.SemaphoreType.DMA((COARSEN + 1,))]

    from_odd, *kept = kernel_call(
        functools.partial(first_sweep, True),
        [narrow, *held],
        [inputs, guess, weights],
        "first_sweep_odd",
        4,
        hbm=(0, 1, 2),
        scratch=scratch,
    )
    left_even = send(from_odd, up_between)
    from_even, own_w, later_w, start = kernel_call(
        functools.partial(first_sweep, False),
        [narrow, *held],
        [inputs, guess, weights, *kept, from_odd],
        "first_sweep_even",
        4,
        hbm=(0, 1, 2),
        scratch=scratch,
        aliases={3: 1, 4: 2, 5: 3},
    )
    left_odd = send(from_even, up_inside)
    even_w = send(own_w, up_inside)

    left_even, start = kernel_call(
        in_order, [narrow, wide], [left_even, start], "even_first", 1, aliases={0: 0, 1: 1}
    )
    rhs, solved, c1 = kernel_call(
        second_sweep_lead,
        [wide, wide, narrow],
        [left_odd, own_w, later_w, start],
        "second_sweep_lead",
        40,
    )
    got3 = send(c1, [(1, 3)])
    rhs_of_even, first, start, solved = kernel_call(
        second_sweep_even,
        [wide, wide, wide, wide],
        [left_even, own_w, later_w, inputs, start, solved],
        "second_sweep_even",
        4,
        hbm=(3,),
        scratch=[pltpu.VMEM((CHANS, CELLS), F32), pltpu.SemaphoreType.DMA(())],
        aliases={4: 2, 5: 3},
    )
    first = send(first, [(4, 5), (8, 9)])
    even_rhs = send(rhs_of_even, up_inside)
    rhs, solved = kernel_call(
        second_sweep_odd,
        [wide, wide],
        [left_odd, own_w, later_w, rhs, solved],
        "second_sweep_odd",
        4,
        aliases={3: 0, 4: 1},
    )
    both = [even_rhs, rhs, even_w, own_w]

    def chained(body, args, name, steps, out=narrow):
        nonlocal solved
        value, solved = kernel_call(
            body, [out, wide], [*args, solved], name, steps, aliases={len(args): 1}
        )
        return value

    def pair(owners, keep, got, name):
        return chained(functools.partial(two_steps, owners, keep), [*both, got], name, 2)

    part = chained(lead_half, [got3, even_w], "lead_first", 10, wide)
    upper1 = chained(lead_rest, [rhs, own_w, even_rhs, part], "relax_lead", 1)
    got4 = send(upper1, [(3, 5)])
    c5 = chained(functools.partial(one_step, (5, 9)), [first, rhs, own_w], "relax_first", 1)
    got3_rest = send(c5, [(5, 7), (9, 11)])
    c5_lead = pair((5,), False, got4, "again_lead")
    got5 = send(c5_lead, [(5, 7)])
    upper7 = pair((7,), False, got3_rest, "relax_rest")
    got4_rest = send(upper7, [(7, 9)])
    upper_prev = send(upper7, [(7, 11)])
    upper11 = pair((11,), False, got3_rest, "relax_last")
    z2 = chained(
        functools.partial(steps_or_copy, 7, True), [upper11, *both, got5], "again_end_lead", 2
    )
    got6 = send(z2, [(7, 11), (11, 15)])
    c9 = chained(
        functools.partial(steps_or_copy, 9, False), [upper11, *both, got4_rest], "again_rest", 2
    )
    got5_rest = send(c9, [(9, 11), (11, 13)])
    base = chained(coarse_base, [upper_prev, own_w], "coarse_base", 1, wide)
    c13 = chained(again_end, [*both, got5_rest], "again_end_rest", 2)
    z3 = chained(lead_step, [got6, base, own_w, got3, got4, z2, c13], "coarse_lead", 1)
    got7 = send(z3, [(11, 13), (7, 9), (13, 15)])
    got7b = send(z3, [(11, 15), (3, 2), (5, 4), (7, 8)])
    c13 = chained(lead_two_steps, [got7, z3, got5, *both], "final_lead", 2)
    got8 = send(c13, [(13, 15), (9, 11)])
    got8b = send(c13, [(13, 14), (9, 10), (11, 12), (7, 6)])
    (solved,) = kernel_call(
        end_step, [wide], [got6, *both, got7, got7b, solved], "coarse_end", 4, aliases={7: 0}
    )
    return kernel_call(
        last_sweep,
        [jax.ShapeDtypeStruct((COARSEN, CHANS, CELLS), F32)],
        [start, got8b, got8, got3, got4, got5, got7, got7b, *both, rhs_of_even, later_w, solved],
        "last_sweep",
        4,
        scratch=[
            pltpu.VMEM(STATE, F32),
            pltpu.VMEM((COARSEN, CHANS, CELLS), F32),
            pltpu.SemaphoreType.DMA((COARSEN,)),
        ],
    )[0]


def solution(mesh):
    return jax.shard_map(
        per_device,
        mesh=mesh,
        in_specs=(P(None, "batch"), P("layer", None, "batch"), P("layer", None, None)),
        out_specs=P("layer", None, "batch"),
        check_vma=False,
    )
```

```python
import functools

import jax
import jax.numpy as jnp
from jax import lax
from jax.experimental import pallas as pl
from jax.experimental.pallas import tpu as pltpu
from jax.sharding import PartitionSpec as P

SIDE = 16
CELLS = 256
CHANS = 256
TAPS = 9 * CHANS
COARSEN = 4
DEVICES = 16
F32 = jnp.float32
BF16 = jnp.bfloat16
STATE = (CELLS, CHANS)
VMEM_LIMIT = 12 << 20


def conv_tanh(state, weight):
    column = lax.broadcasted_iota(jnp.int32, STATE, 0) % SIDE
    before = jnp.where(column == 0, 0.0, pltpu.roll(state, 1, 0)).astype(BF16)
    after = jnp.where(column == SIDE - 1, 0.0, pltpu.roll(state, CELLS - 1, 0)).astype(BF16)
    here = state.astype(BF16)
    edge = jnp.zeros((SIDE, CHANS), BF16)

    def product(piece, row, column):
        if row == 0:
            piece = jnp.concatenate([edge, piece[:-SIDE]], 0)
        if row == 2:
            piece = jnp.concatenate([piece[SIDE:], edge], 0)
        tap = 3 * row + column
        return lax.dot_general(
            piece,
            weight[:, tap * CHANS : (tap + 1) * CHANS],
            (((1,), (1,)), ((), ())),
            preferred_element_type=F32,
        )

    total = product(here, 1, 1)
    for column, piece in ((1, -here), (0, -before), (2, -after)):
        for row in (0, 2) if column == 1 else (1, 0, 2):
            total = total - product(piece, row, column)
    return jnp.tanh(total)


def vmem(shape, dtype):
    return pltpu.VMEM(shape, dtype)


def kernel_call(body, outs, args, name, steps, hbm=(), scratch=(), aliases=None):
    def space(i):
        return pltpu.HBM if i in hbm else pltpu.VMEM

    args = [pltpu.with_memory_space_constraint(a, space(i)) for i, a in enumerate(args)]
    return pl.pallas_call(
        body,
        out_shape=outs,
        in_specs=[pl.BlockSpec(memory_space=space(i)) for i in range(len(args))],
        out_specs=[
            pl.BlockSpec(memory_space=pltpu.VMEM if hasattr(o, "memory_space") else pl.ANY)
            for o in outs
        ],
        scratch_shapes=list(scratch),
        input_output_aliases=aliases or {},
        compiler_params=pltpu.CompilerParams(vmem_limit_bytes=VMEM_LIMIT),
        cost_estimate=pl.CostEstimate(
            flops=steps * 2 * TAPS * CELLS * CHANS, bytes_accessed=1 << 20, transcendentals=0
        ),
        name=name,
    )(*args)


def place():
    return lax.axis_index("layer")


def first_sweep(first, *refs):
    inputs, guess, weights = refs[:3]
    cpoint, own_w, later_w, start, raw, sems = refs[-6:]
    me = place()

    early = (me % 2 == 1) | (me == 0)

    @pl.when(early if first else jnp.logical_not(early))
    def _():
        source = [pltpu.make_async_copy(weights.at[0], own_w, sems.at[1])]
        for i in range(COARSEN - 1):
            source.append(pltpu.make_async_copy(weights.at[i + 1], later_w.at[i], sems.at[i + 2]))
        begin = pltpu.make_async_copy(inputs, raw, sems.at[0])
        other = pltpu.make_async_copy(guess.at[0], raw, sems.at[0])

        @pl.when(me == 0)
        def _():
            begin.start()

        @pl.when(me > 0)
        def _():
            other.start()

        for copy in source:
            copy.start()
        other.wait()
        state = raw[...].T

        @pl.when(me == 0)
        def _():
            start[...] = state

        for i in range(COARSEN):
            source[i].wait()
            state = state + 0.25 * conv_tanh(state, own_w if i == 0 else later_w[i - 1])
        cpoint[...] = state.astype(BF16)

    if not first:

        @pl.when(me == 0)
        def _():
            cpoint[...] = refs[6][...]


def sweep(state, own_w, later_w, rhs):
    terms = []
    for i in range(COARSEN):
        terms.append(conv_tanh(state, own_w if i == 0 else later_w[i - 1]))
        state = state + 0.25 * terms[-1]
    rhs[...] = 0.25 * (terms[0] + terms[1] + terms[2] + terms[3]) - terms[0]
    return state


def second_sweep_lead(left_odd, own_w, later_w, _, rhs, solved, out):
    @pl.when(place() == 1)
    def _():
        out[...] = sweep(left_odd[...].astype(F32), own_w, later_w, rhs).astype(BF16)


def second_sweep_even(left_even, own_w, later_w, inputs, _, __, rhs, first, start, solved, raw, sem):
    me = place()

    @pl.when(me % 2 == 0)
    def _():
        left = jnp.where(me == 0, start[...], left_even[...].astype(F32))
        first[...] = sweep(left, own_w, later_w, rhs)

    @pl.when(me == 1)
    def _():
        copy = pltpu.make_async_copy(inputs, raw, sem)
        copy.start()
        copy.wait()
        start[...] = raw[...].T


def second_sweep_odd(left_odd, own_w, later_w, _, __, rhs, solved):
    me = place()

    @pl.when((me % 2 == 1) & (me > 1))
    def _():
        sweep(left_odd[...].astype(F32), own_w, later_w, rhs)


def in_order(*refs):
    pass


def either(me, owners):
    chosen = me == owners[0]
    for owner in owners[1:]:
        chosen |= me == owner
    return chosen


def both_steps(even_rhs, rhs, even_w, own_w, got):
    value = got[...].astype(F32)
    value = value + conv_tanh(value, even_w) + even_rhs[...]
    return value + conv_tanh(value, own_w) + rhs[...]


def two_steps(owners, keep, even_rhs, rhs, even_w, own_w, got, _, out, solved):
    @pl.when(either(place(), owners))
    def _():
        value = both_steps(even_rhs, rhs, even_w, own_w, got)
        if keep:
            solved[...] = value
        out[...] = value.astype(BF16)


def lead_half(got, even_w, _, out, solved):
    @pl.when(place() == 3)
    def _():
        value = got[...].astype(F32)
        out[...] = value + conv_tanh(value, even_w)


def lead_rest(rhs, own_w, even_rhs, part, _, out, solved):
    @pl.when(place() == 3)
    def _():
        value = part[...] + even_rhs[...]
        value = value + conv_tanh(value, own_w) + rhs[...]
        solved[...] = value
        out[...] = value.astype(BF16)


def one_step(owners, first, rhs, own_w, _, out, solved):
    @pl.when(either(place(), owners))
    def _():
        value = first[...]
        out[...] = (value + conv_tanh(value, own_w) + rhs[...]).astype(BF16)


def coarse_step(got, own_w):
    value = got[...].astype(F32)
    return value + 4.0 * conv_tanh(value, own_w)


def steps_or_copy(owner, keep, upper, even_rhs, rhs, even_w, own_w, got, _, out, solved):
    two_steps((owner,), keep, even_rhs, rhs, even_w, own_w, got, _, out, solved)

    @pl.when(place() == 11)
    def _():
        out[...] = upper[...]


def again_rest(upper, even_rhs, rhs, even_w, own_w, got, _, __, out, solved, passed):
    steps_or_copy(9, False, upper, even_rhs, rhs, even_w, own_w, got, _, out, solved)


def coarse_base(upper, own_w, _, out, solved):
    @pl.when(place() == 11)
    def _():
        out[...] = coarse_step(upper, own_w)


def again_end(even_rhs, rhs, even_w, own_w, got, _, out, solved):
    @pl.when(either(place(), (11, 13)))
    def _():
        value = both_steps(even_rhs, rhs, even_w, own_w, got)
        solved[...] = value
        out[...] = value.astype(BF16)


def lead_step(got, base, own_w, early3, early4, mine, behind, _, out, solved):
    me = place()

    @pl.when(me == 11)
    def _():
        value = coarse_step(got, own_w) + (solved[...] - base[...])
        solved[...] = value
        out[...] = value.astype(BF16)

    for owner, source in ((3, early3), (5, early4), (7, mine), (13, behind)):

        @pl.when(me == owner)
        def _():
            out[...] = source[...]


def lead_two_steps(got, mine, early5, even_rhs, rhs, even_w, own_w, _, out, solved):
    two_steps((9, 13), False, even_rhs, rhs, even_w, own_w, got, _, out, solved)
    for owner, source in ((11, mine), (7, early5)):

        @pl.when(place() == owner)
        def _():
            out[...] = source[...]


def end_step(upper, even_rhs, rhs, even_w, own_w, got, lead, _, solved):
    @pl.when(place() == 15)
    def _():
        value = both_steps(even_rhs, rhs, even_w, own_w, got) - coarse_step(upper, own_w)
        solved[...] = value + coarse_step(lead, own_w)


def last_sweep(
    start, got8b, got8, got3, got4, got5, got7, got7b,
    even_rhs, rhs, even_w, own_w, rhs_of_even, later_w, solved, states, left, ready, sems,
):
    me = place()
    sources = (
        (start, (0, 1)),
        (got7b, (2, 4, 8)),
        (got8b, (6, 10, 12, 14)),
        (got3, (3,)),
        (got4, (5,)),
        (got5, (7,)),
        (got7, (9, 13)),
        (got8, (11, 15)),
    )
    for source, owners in sources:

        @pl.when(either(me, owners))
        def _():
            left[...] = source[...].astype(F32)

    @pl.when(me % 2 == 1)
    def _():
        value = left[...]
        left[...] = value + conv_tanh(value, even_w) + even_rhs[...]

    def store(i, value):
        ready[i] = value.T
        copy = pltpu.make_async_copy(ready.at[i], states.at[i], sems.at[i])
        copy.start()
        return copy

    state = left[...]
    term = conv_tanh(state, own_w)
    own = jnp.where(me % 2 == 0, rhs_of_even[...], rhs[...])
    end = jnp.where(me % 4 == 3, solved[...], state + term + own)
    copies = [store(COARSEN - 1, end)]
    state = state + 0.25 * term
    copies.append(store(0, state))
    for i in range(1, COARSEN - 1):
        state = state + 0.25 * conv_tanh(state, later_w[i - 1])
        copies.append(store(i, state))
    for copy in copies:
        copy.wait()


def per_device(inputs, guess, weights):
    def send(value, pairs):
        return lax.ppermute(value, "layer", pairs)

    narrow = vmem(STATE, BF16)
    wide = vmem(STATE, F32)
    held = [vmem((CHANS, TAPS), BF16), vmem((COARSEN - 1, CHANS, TAPS), BF16), wide]
    up_inside = [(i, i + 1) for i in range(0, DEVICES, 2)]
    up_between = [(i, i + 1) for i in range(1, DEVICES - 1, 2)]
    scratch = [pltpu.VMEM((CHANS, CELLS), F32), pltpu.SemaphoreType.DMA((COARSEN + 1,))]

    from_odd, *kept = kernel_call(
        functools.partial(first_sweep, True),
        [narrow, *held],
        [inputs, guess, weights],
        "first_sweep_odd",
        4,
        hbm=(0, 1, 2),
        scratch=scratch,
    )
    left_even = send(from_odd, up_between)
    from_even, own_w, later_w, start = kernel_call(
        functools.partial(first_sweep, False),
        [narrow, *held],
        [inputs, guess, weights, *kept, from_odd],
        "first_sweep_even",
        4,
        hbm=(0, 1, 2),
        scratch=scratch,
        aliases={3: 1, 4: 2, 5: 3},
    )
    left_odd = send(from_even, up_inside)
    even_w = send(own_w, up_inside)

    left_even, start = kernel_call(
        in_order, [narrow, wide], [left_even, start], "even_first", 1, aliases={0: 0, 1: 1}
    )
    rhs, solved, c1 = kernel_call(
        second_sweep_lead,
        [wide, wide, narrow],
        [left_odd, own_w, later_w, start],
        "second_sweep_lead",
        40,
    )
    got3 = send(c1, [(1, 3)])
    rhs_of_even, first, start, solved = kernel_call(
        second_sweep_even,
        [wide, wide, wide, wide],
        [left_even, own_w, later_w, inputs, start, solved],
        "second_sweep_even",
        4,
        hbm=(3,),
        scratch=[pltpu.VMEM((CHANS, CELLS), F32), pltpu.SemaphoreType.DMA(())],
        aliases={4: 2, 5: 3},
    )
    even_rhs = send(rhs_of_even, up_inside)
    first = send(first, [(4, 5), (8, 9)])
    rhs, solved = kernel_call(
        second_sweep_odd,
        [wide, wide],
        [left_odd, own_w, later_w, rhs, solved],
        "second_sweep_odd",
        0,
        aliases={3: 0, 4: 1},
    )
    both = [even_rhs, rhs, even_w, own_w]

    def chained(body, args, name, steps, out=narrow):
        nonlocal solved
        value, solved = kernel_call(
            body, [out, wide], [*args, solved], name, steps, aliases={len(args): 1}
        )
        return value

    def pair(owners, keep, got, name):
        return chained(functools.partial(two_steps, owners, keep), [*both, got], name, 2)

    part = chained(lead_half, [got3, even_w], "lead_first", 7, wide)
    upper1 = chained(lead_rest, [rhs, own_w, even_rhs, part], "relax_lead", 20)
    got4 = send(upper1, [(3, 5)])
    c5 = chained(functools.partial(one_step, (5, 9)), [first, rhs, own_w], "relax_first", 1)
    got3_rest = send(c5, [(5, 7)])
    got3_last = send(c5, [(9, 11)])
    c5_lead = pair((5,), False, got4, "again_lead")
    got5 = send(c5_lead, [(5, 7)])
    upper7 = pair((7,), False, got3_rest, "relax_rest")
    got4_rest = send(upper7, [(7, 9)])
    upper11 = pair((11,), False, got3_last, "relax_last")
    z2 = chained(
        functools.partial(steps_or_copy, 7, True), [upper11, *both, got5], "again_end_lead", 2
    )
    got6 = send(z2, [(7, 11), (11, 15)])
    c9, solved, upper7 = kernel_call(
        again_rest,
        [narrow, wide, narrow],
        [upper11, *both, got4_rest, solved, upper7],
        "again_rest",
        2,
        aliases={6: 1, 7: 2},
    )
    got5_rest = send(c9, [(9, 11), (11, 13)])
    upper_prev = send(upper7, [(7, 11)])
    c13 = chained(again_end, [*both, got5_rest], "again_end_rest", 2)
    base = chained(coarse_base, [upper_prev, own_w], "coarse_base", 1, wide)
    z3 = chained(lead_step, [got6, base, own_w, got3, got4, z2, c13], "coarse_lead", 1)
    got7 = send(z3, [(11, 13), (7, 9), (13, 15)])
    got7b = send(z3, [(11, 15), (3, 2), (5, 4), (7, 8)])
    c13 = chained(lead_two_steps, [got7, z3, got5, *both], "final_lead", 2)
    got8 = send(c13, [(13, 15), (9, 11)])
    got8b = send(c13, [(13, 14), (9, 10), (11, 12), (7, 6)])
    (solved,) = kernel_call(
        end_step, [wide], [got6, *both, got7, got7b, solved], "coarse_end", 4, aliases={7: 0}
    )
    return kernel_call(
        last_sweep,
        [jax.ShapeDtypeStruct((COARSEN, CHANS, CELLS), F32)],
        [start, got8b, got8, got3, got4, got5, got7, got7b, *both, rhs_of_even, later_w, solved],
        "last_sweep",
        4,
        scratch=[
            pltpu.VMEM(STATE, F32),
            pltpu.VMEM((COARSEN, CHANS, CELLS), F32),
            pltpu.SemaphoreType.DMA((COARSEN,)),
        ],
    )[0]


def solution(mesh):
    return jax.shard_map(
        per_device,
        mesh=mesh,
        in_specs=(P(None, "batch"), P("layer", None, "batch"), P("layer", None, None)),
        out_specs=P("layer", None, "batch"),
        check_vma=False,
    )
```

```python
import functools

import jax
import jax.numpy as jnp
from jax import lax
from jax.experimental import pallas as pl
from jax.experimental.pallas import tpu as pltpu
from jax.sharding import PartitionSpec as P

SIDE = 16
CELLS = 256
CHANS = 256
TAPS = 9 * CHANS
COARSEN = 4
DEVICES = 16
F32 = jnp.float32
BF16 = jnp.bfloat16
STATE = (CELLS, CHANS)
VMEM_LIMIT = 12 << 20


def conv_tanh(state, weight):
    column = lax.broadcasted_iota(jnp.int32, STATE, 0) % SIDE
    before = jnp.where(column == 0, 0.0, pltpu.roll(state, 1, 0)).astype(BF16)
    after = jnp.where(column == SIDE - 1, 0.0, pltpu.roll(state, CELLS - 1, 0)).astype(BF16)
    here = state.astype(BF16)
    edge = jnp.zeros((SIDE, CHANS), BF16)

    def product(piece, row, column):
        if row == 0:
            piece = jnp.concatenate([edge, piece[:-SIDE]], 0)
        if row == 2:
            piece = jnp.concatenate([piece[SIDE:], edge], 0)
        tap = 3 * row + column
        return lax.dot_general(
            piece,
            weight[:, tap * CHANS : (tap + 1) * CHANS],
            (((1,), (1,)), ((), ())),
            preferred_element_type=F32,
        )

    total = product(here, 1, 1)
    for column, piece in ((1, -here), (0, -before), (2, -after)):
        for row in (0, 2) if column == 1 else (1, 0, 2):
            total = total - product(piece, row, column)
    return jnp.tanh(total)


def vmem(shape, dtype):
    return pltpu.VMEM(shape, dtype)


def kernel_call(body, outs, args, name, steps, hbm=(), scratch=(), aliases=None):
    def space(i):
        return pltpu.HBM if i in hbm else pltpu.VMEM

    args = [pltpu.with_memory_space_constraint(a, space(i)) for i, a in enumerate(args)]
    return pl.pallas_call(
        body,
        out_shape=outs,
        in_specs=[pl.BlockSpec(memory_space=space(i)) for i in range(len(args))],
        out_specs=[
            pl.BlockSpec(memory_space=pltpu.VMEM if hasattr(o, "memory_space") else pl.ANY)
            for o in outs
        ],
        scratch_shapes=list(scratch),
        input_output_aliases=aliases or {},
        compiler_params=pltpu.CompilerParams(vmem_limit_bytes=VMEM_LIMIT),
        cost_estimate=pl.CostEstimate(
            flops=steps * 2 * TAPS * CELLS * CHANS, bytes_accessed=1 << 20, transcendentals=0
        ),
        name=name,
    )(*args)


def place():
    return lax.axis_index("layer")


def first_sweep(first, *refs):
    inputs, guess, weights = refs[:3]
    cpoint, own_w, later_w, start, raw, sems = refs[-6:]
    me = place()

    early = (me % 2 == 1) | (me == 0)

    @pl.when(early if first else jnp.logical_not(early))
    def _():
        source = [pltpu.make_async_copy(weights.at[0], own_w, sems.at[1])]
        for i in range(COARSEN - 1):
            source.append(pltpu.make_async_copy(weights.at[i + 1], later_w.at[i], sems.at[i + 2]))
        begin = pltpu.make_async_copy(inputs, raw, sems.at[0])
        other = pltpu.make_async_copy(guess.at[0], raw, sems.at[0])

        @pl.when(me == 0)
        def _():
            begin.start()

        @pl.when(me > 0)
        def _():
            other.start()

        for copy in source:
            copy.start()
        other.wait()
        state = raw[...].T

        @pl.when(me == 0)
        def _():
            start[...] = state

        for i in range(COARSEN):
            source[i].wait()
            state = state + 0.25 * conv_tanh(state, own_w if i == 0 else later_w[i - 1])
        cpoint[...] = state.astype(BF16)

    if not first:

        @pl.when(me == 0)
        def _():
            cpoint[...] = refs[6][...]


def sweep(state, own_w, later_w, rhs):
    terms = []
    for i in range(COARSEN):
        terms.append(conv_tanh(state, own_w if i == 0 else later_w[i - 1]))
        state = state + 0.25 * terms[-1]
    rhs[...] = 0.25 * (terms[0] + terms[1] + terms[2] + terms[3]) - terms[0]
    return state


def second_sweep_lead(left_odd, own_w, later_w, _, rhs, solved, out):
    @pl.when(place() == 1)
    def _():
        out[...] = sweep(left_odd[...].astype(F32), own_w, later_w, rhs).astype(BF16)


def second_sweep_even(left_even, own_w, later_w, inputs, _, __, rhs, first, start, solved, raw, sem):
    me = place()

    @pl.when(me % 2 == 0)
    def _():
        left = jnp.where(me == 0, start[...], left_even[...].astype(F32))
        first[...] = sweep(left, own_w, later_w, rhs)

    @pl.when(me == 1)
    def _():
        copy = pltpu.make_async_copy(inputs, raw, sem)
        copy.start()
        copy.wait()
        start[...] = raw[...].T


def second_sweep_odd(left_odd, own_w, later_w, _, __, rhs, solved):
    me = place()

    @pl.when((me % 2 == 1) & (me > 1))
    def _():
        sweep(left_odd[...].astype(F32), own_w, later_w, rhs)


def in_order(*refs):
    pass


def either(me, owners):
    chosen = me == owners[0]
    for owner in owners[1:]:
        chosen |= me == owner
    return chosen


def both_steps(even_rhs, rhs, even_w, own_w, got):
    value = got[...].astype(F32)
    value = value + conv_tanh(value, even_w) + even_rhs[...]
    return value + conv_tanh(value, own_w) + rhs[...]


def two_steps(owners, keep, even_rhs, rhs, even_w, own_w, got, _, out, solved):
    @pl.when(either(place(), owners))
    def _():
        value = both_steps(even_rhs, rhs, even_w, own_w, got)
        if keep:
            solved[...] = value
        out[...] = value.astype(BF16)


def lead_half(got, even_w, _, out, solved):
    @pl.when(place() == 3)
    def _():
        value = got[...].astype(F32)
        out[...] = value + conv_tanh(value, even_w)


def lead_rest(rhs, own_w, even_rhs, part, _, out, solved):
    @pl.when(place() == 3)
    def _():
        value = part[...] + even_rhs[...]
        value = value + conv_tanh(value, own_w) + rhs[...]
        solved[...] = value
        out[...] = value.astype(BF16)


def one_step(owners, first, rhs, own_w, _, out, solved):
    @pl.when(either(place(), owners))
    def _():
        value = first[...]
        out[...] = (value + conv_tanh(value, own_w) + rhs[...]).astype(BF16)


def coarse_step(got, own_w):
    value = got[...].astype(F32)
    return value + 4.0 * conv_tanh(value, own_w)


def steps_or_copy(owner, keep, upper, even_rhs, rhs, even_w, own_w, got, _, out, solved):
    two_steps((owner,), keep, even_rhs, rhs, even_w, own_w, got, _, out, solved)

    @pl.when(place() == 11)
    def _():
        out[...] = upper[...]


def coarse_base(upper, own_w, _, out, solved):
    @pl.when(place() == 11)
    def _():
        out[...] = coarse_step(upper, own_w)


def again_end(even_rhs, rhs, even_w, own_w, got, _, out, solved):
    @pl.when(either(place(), (11, 13)))
    def _():
        value = both_steps(even_rhs, rhs, even_w, own_w, got)
        solved[...] = value
        out[...] = value.astype(BF16)


def lead_step(got, base, own_w, early3, early4, mine, behind, _, out, solved):
    me = place()

    @pl.when(me == 11)
    def _():
        value = coarse_step(got, own_w) + (solved[...] - base[...])
        solved[...] = value
        out[...] = value.astype(BF16)

    for owner, source in ((3, early3), (5, early4), (7, mine), (13, behind)):

        @pl.when(me == owner)
        def _():
            out[...] = source[...]


def lead_two_steps(got, mine, early5, even_rhs, rhs, even_w, own_w, _, out, solved):
    two_steps((9, 13), False, even_rhs, rhs, even_w, own_w, got, _, out, solved)
    for owner, source in ((11, mine), (7, early5)):

        @pl.when(place() == owner)
        def _():
            out[...] = source[...]


def end_step(upper, even_rhs, rhs, even_w, own_w, got, lead, _, solved):
    @pl.when(place() == 15)
    def _():
        value = both_steps(even_rhs, rhs, even_w, own_w, got) - coarse_step(upper, own_w)
        solved[...] = value + coarse_step(lead, own_w)


def last_sweep(
    start, got8b, got8, got3, got4, got5, got7, got7b,
    even_rhs, rhs, even_w, own_w, rhs_of_even, later_w, solved, states, left, ready, sems,
):
    me = place()
    sources = (
        (start, (0, 1)),
        (got7b, (2, 4, 8)),
        (got8b, (6, 10, 12, 14)),
        (got3, (3,)),
        (got4, (5,)),
        (got5, (7,)),
        (got7, (9, 13)),
        (got8, (11, 15)),
    )
    for source, owners in sources:

        @pl.when(either(me, owners))
        def _():
            left[...] = source[...].astype(F32)

    @pl.when(me % 2 == 1)
    def _():
        value = left[...]
        left[...] = value + conv_tanh(value, even_w) + even_rhs[...]

    def store(i, value):
        ready[i] = value.T
        copy = pltpu.make_async_copy(ready.at[i], states.at[i], sems.at[i])
        copy.start()
        return copy

    state = left[...]
    term = conv_tanh(state, own_w)
    own = jnp.where(me % 2 == 0, rhs_of_even[...], rhs[...])
    end = jnp.where(me % 4 == 3, solved[...], state + term + own)
    copies = [store(COARSEN - 1, end)]
    state = state + 0.25 * term
    copies.append(store(0, state))
    for i in range(1, COARSEN - 1):
        state = state + 0.25 * conv_tanh(state, later_w[i - 1])
        copies.append(store(i, state))
    for copy in copies:
        copy.wait()


def per_device(inputs, guess, weights):
    def send(value, pairs):
        return lax.ppermute(value, "layer", pairs)

    narrow = vmem(STATE, BF16)
    wide = vmem(STATE, F32)
    held = [vmem((CHANS, TAPS), BF16), vmem((COARSEN - 1, CHANS, TAPS), BF16), wide]
    up_inside = [(i, i + 1) for i in range(0, DEVICES, 2)]
    up_between = [(i, i + 1) for i in range(1, DEVICES - 1, 2)]
    scratch = [pltpu.VMEM((CHANS, CELLS), F32), pltpu.SemaphoreType.DMA((COARSEN + 1,))]

    from_odd, *kept = kernel_call(
        functools.partial(first_sweep, True),
        [narrow, *held],
        [inputs, guess, weights],
        "first_sweep_odd",
        4,
        hbm=(0, 1, 2),
        scratch=scratch,
    )
    left_even = send(from_odd, up_between)
    from_even, own_w, later_w, start = kernel_call(
        functools.partial(first_sweep, False),
        [narrow, *held],
        [inputs, guess, weights, *kept, from_odd],
        "first_sweep_even",
        4,
        hbm=(0, 1, 2),
        scratch=scratch,
        aliases={3: 1, 4: 2, 5: 3},
    )
    left_odd = send(from_even, up_inside)
    even_w = send(own_w, up_inside)

    left_even, start = kernel_call(
        in_order, [narrow, wide], [left_even, start], "even_first", 1, aliases={0: 0, 1: 1}
    )
    rhs, solved, c1 = kernel_call(
        second_sweep_lead,
        [wide, wide, narrow],
        [left_odd, own_w, later_w, start],
        "second_sweep_lead",
        40,
    )
    got3 = send(c1, [(1, 3)])
    rhs_of_even, first, start, solved = kernel_call(
        second_sweep_even,
        [wide, wide, wide, wide],
        [left_even, own_w, later_w, inputs, start, solved],
        "second_sweep_even",
        4,
        hbm=(3,),
        scratch=[pltpu.VMEM((CHANS, CELLS), F32), pltpu.SemaphoreType.DMA(())],
        aliases={4: 2, 5: 3},
    )
    even_rhs = send(rhs_of_even, up_inside)
    first = send(first, [(4, 5), (8, 9)])
    rhs, solved = kernel_call(
        second_sweep_odd,
        [wide, wide],
        [left_odd, own_w, later_w, rhs, solved],
        "second_sweep_odd",
        0,
        aliases={3: 0, 4: 1},
    )
    both = [even_rhs, rhs, even_w, own_w]

    def chained(body, args, name, steps, out=narrow):
        nonlocal solved
        value, solved = kernel_call(
            body, [out, wide], [*args, solved], name, steps, aliases={len(args): 1}
        )
        return value

    def pair(owners, keep, got, name):
        return chained(functools.partial(two_steps, owners, keep), [*both, got], name, 2)

    part = chained(lead_half, [got3, even_w], "lead_first", 7, wide)
    upper1 = chained(lead_rest, [rhs, own_w, even_rhs, part], "relax_lead", 20)
    got4 = send(upper1, [(3, 5)])
    c5 = chained(functools.partial(one_step, (5, 9)), [first, rhs, own_w], "relax_first", 1)
    got3_rest = send(c5, [(5, 7)])
    got3_last = send(c5, [(9, 11)])
    c5_lead = pair((5,), False, got4, "again_lead")
    got5 = send(c5_lead, [(5, 7)])
    upper7 = pair((7,), False, got3_rest, "relax_rest")
    got4_rest = send(upper7, [(7, 9)])
    upper_prev = send(upper7, [(7, 11)])
    upper11 = pair((11,), False, got3_last, "relax_last")
    z2 = chained(
        functools.partial(steps_or_copy, 7, True), [upper11, *both, got5], "again_end_lead", 2
    )
    got6 = send(z2, [(7, 11), (11, 15)])
    c9 = chained(
        functools.partial(steps_or_copy, 9, False), [upper11, *both, got4_rest], "again_rest", 2
    )
    got5_rest = send(c9, [(9, 11), (11, 13)])
    base = chained(coarse_base, [upper_prev, own_w], "coarse_base", 1, wide)
    c13 = chained(again_end, [*both, got5_rest], "again_end_rest", 2)
    z3 = chained(lead_step, [got6, base, own_w, got3, got4, z2, c13], "coarse_lead", 1)
    got7 = send(z3, [(11, 13), (7, 9), (13, 15)])
    got7b = send(z3, [(11, 15), (3, 2), (5, 4), (7, 8)])
    c13 = chained(lead_two_steps, [got7, z3, got5, *both], "final_lead", 2)
    got8 = send(c13, [(13, 15), (9, 11)])
    got8b = send(c13, [(13, 14), (9, 10), (11, 12), (7, 6)])
    (solved,) = kernel_call(
        end_step, [wide], [got6, *both, got7, got7b, solved], "coarse_end", 4, aliases={7: 0}
    )
    return kernel_call(
        last_sweep,
        [jax.ShapeDtypeStruct((COARSEN, CHANS, CELLS), F32)],
        [start, got8b, got8, got3, got4, got5, got7, got7b, *both, rhs_of_even, later_w, solved],
        "last_sweep",
        4,
        scratch=[
            pltpu.VMEM(STATE, F32),
            pltpu.VMEM((COARSEN, CHANS, CELLS), F32),
            pltpu.SemaphoreType.DMA((COARSEN,)),
        ],
    )[0]


def solution(mesh):
    return jax.shard_map(
        per_device,
        mesh=mesh,
        in_specs=(P(None, "batch"), P("layer", None, "batch"), P("layer", None, None)),
        out_specs=P("layer", None, "batch"),
        check_vma=False,
    )
```

```python
import functools

import jax
import jax.numpy as jnp
from jax import lax
from jax.experimental import pallas as pl
from jax.experimental.pallas import tpu as pltpu
from jax.sharding import PartitionSpec as P

SIDE = 16
CELLS = 256
CHANS = 256
TAPS = 9 * CHANS
COARSEN = 4
DEVICES = 16
F32 = jnp.float32
BF16 = jnp.bfloat16
STATE = (CELLS, CHANS)
VMEM_LIMIT = 12 << 20


def conv_tanh(state, weight):
    column = lax.broadcasted_iota(jnp.int32, STATE, 0) % SIDE
    before = jnp.where(column == 0, 0.0, pltpu.roll(state, 1, 0)).astype(BF16)
    after = jnp.where(column == SIDE - 1, 0.0, pltpu.roll(state, CELLS - 1, 0)).astype(BF16)
    here = state.astype(BF16)
    edge = jnp.zeros((SIDE, CHANS), BF16)

    def product(piece, row, column):
        if row == 0:
            piece = jnp.concatenate([edge, piece[:-SIDE]], 0)
        if row == 2:
            piece = jnp.concatenate([piece[SIDE:], edge], 0)
        tap = 3 * row + column
        return lax.dot_general(
            piece,
            weight[:, tap * CHANS : (tap + 1) * CHANS],
            (((1,), (1,)), ((), ())),
            preferred_element_type=F32,
        )

    total = product(here, 1, 1)
    for column, piece in ((1, -here), (0, -before), (2, -after)):
        for row in (0, 2) if column == 1 else (1, 0, 2):
            total = total - product(piece, row, column)
    return jnp.tanh(total)


def vmem(shape, dtype):
    return pltpu.VMEM(shape, dtype)


def kernel_call(body, outs, args, name, steps, hbm=(), scratch=(), aliases=None):
    def space(i):
        return pltpu.HBM if i in hbm else pltpu.VMEM

    args = [pltpu.with_memory_space_constraint(a, space(i)) for i, a in enumerate(args)]
    return pl.pallas_call(
        body,
        out_shape=outs,
        in_specs=[pl.BlockSpec(memory_space=space(i)) for i in range(len(args))],
        out_specs=[
            pl.BlockSpec(memory_space=pltpu.VMEM if hasattr(o, "memory_space") else pl.ANY)
            for o in outs
        ],
        scratch_shapes=list(scratch),
        input_output_aliases=aliases or {},
        compiler_params=pltpu.CompilerParams(vmem_limit_bytes=VMEM_LIMIT),
        cost_estimate=pl.CostEstimate(
            flops=steps * 2 * TAPS * CELLS * CHANS, bytes_accessed=1 << 20, transcendentals=0
        ),
        name=name,
    )(*args)


def place():
    return lax.axis_index("layer")


def first_sweep(first, *refs):
    inputs, guess, weights = refs[:3]
    cpoint, own_w, later_w, start, raw, sems = refs[-6:]
    me = place()

    early = (me % 2 == 1) | (me == 0)

    @pl.when(early if first else jnp.logical_not(early))
    def _():
        source = [pltpu.make_async_copy(weights.at[0], own_w, sems.at[1])]
        for i in range(COARSEN - 1):
            source.append(pltpu.make_async_copy(weights.at[i + 1], later_w.at[i], sems.at[i + 2]))
        begin = pltpu.make_async_copy(inputs, raw, sems.at[0])
        other = pltpu.make_async_copy(guess.at[0], raw, sems.at[0])

        @pl.when(me == 0)
        def _():
            begin.start()

        @pl.when(me > 0)
        def _():
            other.start()

        for copy in source:
            copy.start()
        other.wait()
        state = raw[...].T

        @pl.when(me == 0)
        def _():
            start[...] = state

        for i in range(COARSEN):
            source[i].wait()
            state = state + 0.25 * conv_tanh(state, own_w if i == 0 else later_w[i - 1])
        cpoint[...] = state.astype(BF16)

    if not first:

        @pl.when(me == 0)
        def _():
            cpoint[...] = refs[6][...]


def sweep(state, own_w, later_w, rhs):
    terms = []
    for i in range(COARSEN):
        terms.append(conv_tanh(state, own_w if i == 0 else later_w[i - 1]))
        state = state + 0.25 * terms[-1]
    rhs[...] = 0.25 * (terms[0] + terms[1] + terms[2] + terms[3]) - terms[0]
    return state


def second_sweep_lead(left_odd, own_w, later_w, _, rhs, solved, out):
    @pl.when(place() == 1)
    def _():
        out[...] = sweep(left_odd[...].astype(F32), own_w, later_w, rhs).astype(BF16)


def second_sweep_even(left_even, own_w, later_w, inputs, _, __, rhs, first, start, solved, raw, sem):
    me = place()

    @pl.when(me % 2 == 0)
    def _():
        left = jnp.where(me == 0, start[...], left_even[...].astype(F32))
        first[...] = sweep(left, own_w, later_w, rhs)

    @pl.when(me == 1)
    def _():
        copy = pltpu.make_async_copy(inputs, raw, sem)
        copy.start()
        copy.wait()
        start[...] = raw[...].T


def second_sweep_odd(left_odd, own_w, later_w, _, __, rhs, solved):
    me = place()

    @pl.when((me % 2 == 1) & (me > 1))
    def _():
        sweep(left_odd[...].astype(F32), own_w, later_w, rhs)


def in_order(*refs):
    pass


def either(me, owners):
    chosen = me == owners[0]
    for owner in owners[1:]:
        chosen |= me == owner
    return chosen


def both_steps(even_rhs, rhs, even_w, own_w, got):
    value = got[...].astype(F32)
    value = value + conv_tanh(value, even_w) + even_rhs[...]
    return value + conv_tanh(value, own_w) + rhs[...]


def two_steps(owners, keep, even_rhs, rhs, even_w, own_w, got, _, out, solved):
    @pl.when(either(place(), owners))
    def _():
        value = both_steps(even_rhs, rhs, even_w, own_w, got)
        if keep:
            solved[...] = value
        out[...] = value.astype(BF16)


def lead_half(got, even_w, _, out, solved):
    @pl.when(place() == 3)
    def _():
        value = got[...].astype(F32)
        out[...] = value + conv_tanh(value, even_w)


def lead_rest(rhs, own_w, even_rhs, part, _, out, solved):
    @pl.when(place() == 3)
    def _():
        value = part[...] + even_rhs[...]
        value = value + conv_tanh(value, own_w) + rhs[...]
        solved[...] = value
        out[...] = value.astype(BF16)


def one_step(owners, first, rhs, own_w, _, out, solved):
    @pl.when(either(place(), owners))
    def _():
        value = first[...]
        out[...] = (value + conv_tanh(value, own_w) + rhs[...]).astype(BF16)


def coarse_step(got, own_w):
    value = got[...].astype(F32)
    return value + 4.0 * conv_tanh(value, own_w)


def steps_or_copy(owner, keep, upper, even_rhs, rhs, even_w, own_w, got, _, out, solved):
    two_steps((owner,), keep, even_rhs, rhs, even_w, own_w, got, _, out, solved)

    @pl.when(place() == 11)
    def _():
        out[...] = upper[...]


def coarse_base(upper, own_w, _, out, solved):
    @pl.when(place() == 11)
    def _():
        out[...] = coarse_step(upper, own_w)


def lead_base(base, own_w, lead, _, out, solved):
    @pl.when(place() == 11)
    def _():
        out[...] = coarse_step(lead, own_w) - base[...]


def again_end(even_rhs, rhs, even_w, own_w, base, early3, early4, mine, got, _, out, solved):
    me = place()

    @pl.when(either(me, (11, 13)))
    def _():
        value = both_steps(even_rhs, rhs, even_w, own_w, got)
        value = value + jnp.where(me == 11, base[...], 0.0)
        solved[...] = value
        out[...] = value.astype(BF16)

    for owner, source in ((3, early3), (5, early4), (7, mine)):

        @pl.when(me == owner)
        def _():
            out[...] = source[...]


def lead_two_steps(got, mine, early5, even_rhs, rhs, even_w, own_w, _, out, solved):
    two_steps((9, 13), False, even_rhs, rhs, even_w, own_w, got, _, out, solved)
    for owner, source in ((11, mine), (7, early5)):

        @pl.when(place() == owner)
        def _():
            out[...] = source[...]


def end_step(upper, even_rhs, rhs, even_w, own_w, got, lead, _, solved):
    @pl.when(place() == 15)
    def _():
        value = both_steps(even_rhs, rhs, even_w, own_w, got) - coarse_step(upper, own_w)
        solved[...] = value + coarse_step(lead, own_w)


def last_sweep(
    start, got8b, got8, got3, got4, got5, got7, got7b,
    even_rhs, rhs, even_w, own_w, rhs_of_even, later_w, solved, states, left, ready, sems,
):
    me = place()
    sources = (
        (start, (0, 1)),
        (got7b, (2, 4, 8)),
        (got8b, (6, 10, 12, 14)),
        (got3, (3,)),
        (got4, (5,)),
        (got5, (7,)),
        (got7, (9, 13)),
        (got8, (11, 15)),
    )
    for source, owners in sources:

        @pl.when(either(me, owners))
        def _():
            left[...] = source[...].astype(F32)

    @pl.when(me % 2 == 1)
    def _():
        value = left[...]
        left[...] = value + conv_tanh(value, even_w) + even_rhs[...]

    def store(i, value):
        ready[i] = value.T
        copy = pltpu.make_async_copy(ready.at[i], states.at[i], sems.at[i])
        copy.start()
        return copy

    state = left[...]
    term = conv_tanh(state, own_w)
    own = jnp.where(me % 2 == 0, rhs_of_even[...], rhs[...])
    end = jnp.where(me % 4 == 3, solved[...], state + term + own)
    copies = [store(COARSEN - 1, end)]
    state = state + 0.25 * term
    copies.append(store(0, state))
    for i in range(1, COARSEN - 1):
        state = state + 0.25 * conv_tanh(state, later_w[i - 1])
        copies.append(store(i, state))
    for copy in copies:
        copy.wait()


def per_device(inputs, guess, weights):
    def send(value, pairs):
        return lax.ppermute(value, "layer", pairs)

    narrow = vmem(STATE, BF16)
    wide = vmem(STATE, F32)
    held = [vmem((CHANS, TAPS), BF16), vmem((COARSEN - 1, CHANS, TAPS), BF16), wide]
    up_inside = [(i, i + 1) for i in range(0, DEVICES, 2)]
    up_between = [(i, i + 1) for i in range(1, DEVICES - 1, 2)]
    scratch = [pltpu.VMEM((CHANS, CELLS), F32), pltpu.SemaphoreType.DMA((COARSEN + 1,))]

    from_odd, *kept = kernel_call(
        functools.partial(first_sweep, True),
        [narrow, *held],
        [inputs, guess, weights],
        "first_sweep_odd",
        4,
        hbm=(0, 1, 2),
        scratch=scratch,
    )
    left_even = send(from_odd, up_between)
    from_even, own_w, later_w, start = kernel_call(
        functools.partial(first_sweep, False),
        [narrow, *held],
        [inputs, guess, weights, *kept, from_odd],
        "first_sweep_even",
        4,
        hbm=(0, 1, 2),
        scratch=scratch,
        aliases={3: 1, 4: 2, 5: 3},
    )
    left_odd = send(from_even, up_inside)
    even_w = send(own_w, up_inside)

    left_even, start = kernel_call(
        in_order, [narrow, wide], [left_even, start], "even_first", 1, aliases={0: 0, 1: 1}
    )
    rhs, solved, c1 = kernel_call(
        second_sweep_lead,
        [wide, wide, narrow],
        [left_odd, own_w, later_w, start],
        "second_sweep_lead",
        40,
    )
    got3 = send(c1, [(1, 3)])
    rhs_of_even, first, start, solved = kernel_call(
        second_sweep_even,
        [wide, wide, wide, wide],
        [left_even, own_w, later_w, inputs, start, solved],
        "second_sweep_even",
        4,
        hbm=(3,),
        scratch=[pltpu.VMEM((CHANS, CELLS), F32), pltpu.SemaphoreType.DMA(())],
        aliases={4: 2, 5: 3},
    )
    even_rhs = send(rhs_of_even, up_inside)
    first = send(first, [(4, 5), (8, 9)])
    rhs, solved = kernel_call(
        second_sweep_odd,
        [wide, wide],
        [left_odd, own_w, later_w, rhs, solved],
        "second_sweep_odd",
        0,
        aliases={3: 0, 4: 1},
    )
    both = [even_rhs, rhs, even_w, own_w]

    def chained(body, args, name, steps, out=narrow):
        nonlocal solved
        value, solved = kernel_call(
            body, [out, wide], [*args, solved], name, steps, aliases={len(args): 1}
        )
        return value

    def pair(owners, keep, got, name):
        return chained(functools.partial(two_steps, owners, keep), [*both, got], name, 2)

    part = chained(lead_half, [got3, even_w], "lead_first", 7, wide)
    upper1 = chained(lead_rest, [rhs, own_w, even_rhs, part], "relax_lead", 20)
    got4 = send(upper1, [(3, 5)])
    c5 = chained(functools.partial(one_step, (5, 9)), [first, rhs, own_w], "relax_first", 1)
    got3_rest = send(c5, [(5, 7)])
    got3_last = send(c5, [(9, 11)])
    c5_lead = pair((5,), False, got4, "again_lead")
    got5 = send(c5_lead, [(5, 7)])
    upper7 = pair((7,), False, got3_rest, "relax_rest")
    got4_rest = send(upper7, [(7, 9)])
    upper_prev = send(upper7, [(7, 11)])
    upper11 = pair((11,), False, got3_last, "relax_last")
    z2 = chained(
        functools.partial(steps_or_copy, 7, True), [upper11, *both, got5], "again_end_lead", 2
    )
    got6 = send(z2, [(7, 11), (11, 15)])
    c9 = chained(
        functools.partial(steps_or_copy, 9, False), [upper11, *both, got4_rest], "again_rest", 2
    )
    got5_rest = send(c9, [(9, 11), (11, 13)])
    base = chained(coarse_base, [upper_prev, own_w], "coarse_base", 1, wide)
    base = chained(lead_base, [base, own_w, got6], "lead_base", 10, wide)
    z3 = chained(again_end, [*both, base, got3, got4, z2, got5_rest], "again_end_rest", 2)
    got7 = send(z3, [(11, 13), (7, 9), (13, 15)])
    got7b = send(z3, [(11, 15), (3, 2), (5, 4), (7, 8)])
    c13 = chained(lead_two_steps, [got7, z3, got5, *both], "final_lead", 2)
    got8 = send(c13, [(13, 15), (9, 11)])
    got8b = send(c13, [(13, 14), (9, 10), (11, 12), (7, 6)])
    (solved,) = kernel_call(
        end_step, [wide], [got6, *both, got7, got7b, solved], "coarse_end", 4, aliases={7: 0}
    )
    return kernel_call(
        last_sweep,
        [jax.ShapeDtypeStruct((COARSEN, CHANS, CELLS), F32)],
        [start, got8b, got8, got3, got4, got5, got7, got7b, *both, rhs_of_even, later_w, solved],
        "last_sweep",
        4,
        scratch=[
            pltpu.VMEM(STATE, F32),
            pltpu.VMEM((COARSEN, CHANS, CELLS), F32),
            pltpu.SemaphoreType.DMA((COARSEN,)),
        ],
    )[0]


def solution(mesh):
    return jax.shard_map(
        per_device,
        mesh=mesh,
        in_specs=(P(None, "batch"), P("layer", None, "batch"), P("layer", None, None)),
        out_specs=P("layer", None, "batch"),
        check_vma=False,
    )
```

```python
import functools

import jax
import jax.numpy as jnp
from jax import lax
from jax.experimental import pallas as pl
from jax.experimental.pallas import tpu as pltpu
from jax.sharding import PartitionSpec as P

SIDE = 16
CELLS = 256
CHANS = 256
TAPS = 9 * CHANS
COARSEN = 4
DEVICES = 16
F32 = jnp.float32
BF16 = jnp.bfloat16
STATE = (CELLS, CHANS)
VMEM_LIMIT = 12 << 20


def conv_tanh(state, weight):
    column = lax.broadcasted_iota(jnp.int32, STATE, 0) % SIDE
    before = jnp.where(column == 0, 0.0, pltpu.roll(state, 1, 0)).astype(BF16)
    after = jnp.where(column == SIDE - 1, 0.0, pltpu.roll(state, CELLS - 1, 0)).astype(BF16)
    here = state.astype(BF16)
    edge = jnp.zeros((SIDE, CHANS), BF16)

    def product(piece, row, column):
        if row == 0:
            piece = jnp.concatenate([edge, piece[:-SIDE]], 0)
        if row == 2:
            piece = jnp.concatenate([piece[SIDE:], edge], 0)
        tap = 3 * row + column
        return lax.dot_general(
            piece,
            weight[:, tap * CHANS : (tap + 1) * CHANS],
            (((1,), (1,)), ((), ())),
            preferred_element_type=F32,
        )

    total = product(here, 1, 1)
    for column, piece in ((1, -here), (0, -before), (2, -after)):
        for row in (0, 2) if column == 1 else (1, 0, 2):
            total = total - product(piece, row, column)
    return jnp.tanh(total)


def vmem(shape, dtype):
    return pltpu.VMEM(shape, dtype)


def kernel_call(body, outs, args, name, steps, hbm=(), scratch=(), aliases=None):
    def space(i):
        return pltpu.HBM if i in hbm else pltpu.VMEM

    args = [pltpu.with_memory_space_constraint(a, space(i)) for i, a in enumerate(args)]
    return pl.pallas_call(
        body,
        out_shape=outs,
        in_specs=[pl.BlockSpec(memory_space=space(i)) for i in range(len(args))],
        out_specs=[
            pl.BlockSpec(memory_space=pltpu.VMEM if hasattr(o, "memory_space") else pl.ANY)
            for o in outs
        ],
        scratch_shapes=list(scratch),
        input_output_aliases=aliases or {},
        compiler_params=pltpu.CompilerParams(vmem_limit_bytes=VMEM_LIMIT),
        cost_estimate=pl.CostEstimate(
            flops=steps * 2 * TAPS * CELLS * CHANS, bytes_accessed=1 << 20, transcendentals=0
        ),
        name=name,
    )(*args)


def place():
    return lax.axis_index("layer")


def first_sweep(first, *refs):
    inputs, guess, weights = refs[:3]
    cpoint, own_w, later_w, start, raw, sems = refs[-6:]
    me = place()

    early = (me % 2 == 1) | (me == 0)

    @pl.when(early if first else jnp.logical_not(early))
    def _():
        source = [pltpu.make_async_copy(weights.at[0], own_w, sems.at[1])]
        for i in range(COARSEN - 1):
            source.append(pltpu.make_async_copy(weights.at[i + 1], later_w.at[i], sems.at[i + 2]))
        begin = pltpu.make_async_copy(inputs, raw, sems.at[0])
        other = pltpu.make_async_copy(guess.at[0], raw, sems.at[0])

        @pl.when(me == 0)
        def _():
            begin.start()

        @pl.when(me > 0)
        def _():
            other.start()

        for copy in source:
            copy.start()
        other.wait()
        state = raw[...].T

        @pl.when(me == 0)
        def _():
            start[...] = state

        for i in range(COARSEN):
            source[i].wait()
            state = state + 0.25 * conv_tanh(state, own_w if i == 0 else later_w[i - 1])
        cpoint[...] = state.astype(BF16)

    if not first:

        @pl.when(me == 0)
        def _():
            cpoint[...] = refs[6][...]


def sweep(state, own_w, later_w, rhs):
    terms = []
    for i in range(COARSEN):
        terms.append(conv_tanh(state, own_w if i == 0 else later_w[i - 1]))
        state = state + 0.25 * terms[-1]
    rhs[...] = 0.25 * (terms[0] + terms[1] + terms[2] + terms[3]) - terms[0]
    return state


def second_sweep_lead(left_odd, own_w, later_w, _, rhs, solved, out):
    @pl.when(place() == 1)
    def _():
        out[...] = sweep(left_odd[...].astype(F32), own_w, later_w, rhs).astype(BF16)


def second_sweep_even(left_even, own_w, later_w, inputs, _, __, rhs, first, start, solved, raw, sem):
    me = place()

    @pl.when(me % 2 == 0)
    def _():
        left = jnp.where(me == 0, start[...], left_even[...].astype(F32))
        first[...] = sweep(left, own_w, later_w, rhs)

    @pl.when(me == 1)
    def _():
        copy = pltpu.make_async_copy(inputs, raw, sem)
        copy.start()
        copy.wait()
        start[...] = raw[...].T


def second_sweep_odd(left_odd, own_w, later_w, _, __, rhs, solved):
    me = place()

    @pl.when((me % 2 == 1) & (me > 1))
    def _():
        sweep(left_odd[...].astype(F32), own_w, later_w, rhs)


def in_order(*refs):
    pass


def either(me, owners):
    chosen = me == owners[0]
    for owner in owners[1:]:
        chosen |= me == owner
    return chosen


def both_steps(even_rhs, rhs, even_w, own_w, got):
    value = got[...].astype(F32)
    value = value + conv_tanh(value, even_w) + even_rhs[...]
    return value + conv_tanh(value, own_w) + rhs[...]


def two_steps(owners, keep, even_rhs, rhs, even_w, own_w, got, _, out, solved):
    @pl.when(either(place(), owners))
    def _():
        value = both_steps(even_rhs, rhs, even_w, own_w, got)
        if keep:
            solved[...] = value
        out[...] = value.astype(BF16)


def lead_half(got, even_w, _, out, solved):
    @pl.when(place() == 3)
    def _():
        value = got[...].astype(F32)
        out[...] = value + conv_tanh(value, even_w)


def lead_rest(rhs, own_w, even_rhs, part, _, out, solved):
    @pl.when(place() == 3)
    def _():
        value = part[...] + even_rhs[...]
        value = value + conv_tanh(value, own_w) + rhs[...]
        solved[...] = value
        out[...] = value.astype(BF16)


def one_step(owners, first, rhs, own_w, _, out, solved):
    @pl.when(either(place(), owners))
    def _():
        value = first[...]
        out[...] = (value + conv_tanh(value, own_w) + rhs[...]).astype(BF16)


def coarse_step(got, own_w):
    value = got[...].astype(F32)
    return value + 4.0 * conv_tanh(value, own_w)


def steps_or_copy(owner, copier, other, even_rhs, rhs, even_w, own_w, got, _, out, solved):
    two_steps((owner,), False, even_rhs, rhs, even_w, own_w, got, _, out, solved)

    @pl.when(place() == copier)
    def _():
        out[...] = other[...]


def coarse_base(upper, own_w, _, out, solved):
    @pl.when(place() == 11)
    def _():
        out[...] = coarse_step(upper, own_w)


def lead_base(base, own_w, lead, _, out, solved):
    @pl.when(place() == 11)
    def _():
        out[...] = coarse_step(lead, own_w) - base[...]


def again_end(even_rhs, rhs, even_w, own_w, base, early3, early4, mine, got, _, out, solved):
    me = place()

    @pl.when(either(me, (11, 13)))
    def _():
        value = both_steps(even_rhs, rhs, even_w, own_w, got)
        value = value + jnp.where(me == 11, base[...], 0.0)
        solved[...] = value
        out[...] = value.astype(BF16)

    for owner, source in ((3, early3), (5, early4), (7, mine)):

        @pl.when(me == owner)
        def _():
            out[...] = source[...]


def lead_two_steps(mine, early5, even_rhs, rhs, even_w, own_w, rest, got, _, out, solved):
    two_steps((9,), False, even_rhs, rhs, even_w, own_w, rest, _, out, solved)
    two_steps((13,), False, even_rhs, rhs, even_w, own_w, got, _, out, solved)
    for owner, source in ((11, mine), (7, early5)):

        @pl.when(place() == owner)
        def _():
            out[...] = source[...]


def end_step(upper, even_rhs, rhs, even_w, own_w, got, lead, _, solved):
    @pl.when(place() == 15)
    def _():
        value = both_steps(even_rhs, rhs, even_w, own_w, got) - coarse_step(upper, own_w)
        solved[...] = value + coarse_step(lead, own_w)


def last_sweep(
    start, got8b, got8, got3, got4, got5, got6, got7, got7b,
    even_rhs, rhs, even_w, own_w, rhs_of_even, later_w, solved, states, left, ready, sems,
):
    me = place()
    sources = (
        (start, (0, 1)),
        (got7b, (2, 4, 8)),
        (got8b, (6, 10, 12, 14)),
        (got3, (3,)),
        (got4, (5,)),
        (got5, (7,)),
        (got6, (9,)),
        (got7, (13,)),
        (got8, (11, 15)),
    )
    for source, owners in sources:

        @pl.when(either(me, owners))
        def _():
            left[...] = source[...].astype(F32)

    @pl.when(me % 2 == 1)
    def _():
        value = left[...]
        left[...] = value + conv_tanh(value, even_w) + even_rhs[...]

    def store(i, value):
        ready[i] = value.T
        copy = pltpu.make_async_copy(ready.at[i], states.at[i], sems.at[i])
        copy.start()
        return copy

    state = left[...]
    term = conv_tanh(state, own_w)
    own = jnp.where(me % 2 == 0, rhs_of_even[...], rhs[...])
    end = jnp.where(me % 4 == 3, solved[...], state + term + own)
    copies = [store(COARSEN - 1, end)]
    state = state + 0.25 * term
    copies.append(store(0, state))
    for i in range(1, COARSEN - 1):
        state = state + 0.25 * conv_tanh(state, later_w[i - 1])
        copies.append(store(i, state))
    for copy in copies:
        copy.wait()


def per_device(inputs, guess, weights):
    def send(value, pairs):
        return lax.ppermute(value, "layer", pairs)

    narrow = vmem(STATE, BF16)
    wide = vmem(STATE, F32)
    held = [vmem((CHANS, TAPS), BF16), vmem((COARSEN - 1, CHANS, TAPS), BF16), wide]
    up_inside = [(i, i + 1) for i in range(0, DEVICES, 2)]
    up_between = [(i, i + 1) for i in range(1, DEVICES - 1, 2)]
    scratch = [pltpu.VMEM((CHANS, CELLS), F32), pltpu.SemaphoreType.DMA((COARSEN + 1,))]

    from_odd, *kept = kernel_call(
        functools.partial(first_sweep, True),
        [narrow, *held],
        [inputs, guess, weights],
        "first_sweep_odd",
        4,
        hbm=(0, 1, 2),
        scratch=scratch,
    )
    left_even = send(from_odd, up_between)
    from_even, own_w, later_w, start = kernel_call(
        functools.partial(first_sweep, False),
        [narrow, *held],
        [inputs, guess, weights, *kept, from_odd],
        "first_sweep_even",
        4,
        hbm=(0, 1, 2),
        scratch=scratch,
        aliases={3: 1, 4: 2, 5: 3},
    )
    left_odd = send(from_even, up_inside)
    even_w = send(own_w, up_inside)

    left_even, start = kernel_call(
        in_order, [narrow, wide], [left_even, start], "even_first", 1, aliases={0: 0, 1: 1}
    )
    rhs, solved, c1 = kernel_call(
        second_sweep_lead,
        [wide, wide, narrow],
        [left_odd, own_w, later_w, start],
        "second_sweep_lead",
        40,
    )
    got3 = send(c1, [(1, 3)])
    rhs_of_even, first, start, solved = kernel_call(
        second_sweep_even,
        [wide, wide, wide, wide],
        [left_even, own_w, later_w, inputs, start, solved],
        "second_sweep_even",
        4,
        hbm=(3,),
        scratch=[pltpu.VMEM((CHANS, CELLS), F32), pltpu.SemaphoreType.DMA(())],
        aliases={4: 2, 5: 3},
    )
    even_rhs = send(rhs_of_even, up_inside)
    first = send(first, [(4, 5), (8, 9)])
    rhs, solved = kernel_call(
        second_sweep_odd,
        [wide, wide],
        [left_odd, own_w, later_w, rhs, solved],
        "second_sweep_odd",
        0,
        aliases={3: 0, 4: 1},
    )
    both = [even_rhs, rhs, even_w, own_w]

    def chained(body, args, name, steps, out=narrow):
        nonlocal solved
        value, solved = kernel_call(
            body, [out, wide], [*args, solved], name, steps, aliases={len(args): 1}
        )
        return value

    def pair(owners, keep, got, name):
        return chained(functools.partial(two_steps, owners, keep), [*both, got], name, 2)

    part = chained(lead_half, [got3, even_w], "lead_first", 7, wide)
    upper1 = chained(lead_rest, [rhs, own_w, even_rhs, part], "relax_lead", 20)
    got4 = send(upper1, [(3, 5)])
    c5 = chained(functools.partial(one_step, (5, 9)), [first, rhs, own_w], "relax_first", 1)
    got3_rest = send(c5, [(5, 7)])
    got3_last = send(c5, [(9, 11)])
    c5_lead = pair((5,), False, got4, "again_lead")
    got5 = send(c5_lead, [(5, 7)])
    upper7 = pair((7,), False, got3_rest, "relax_rest")
    got4_rest = send(upper7, [(7, 9)])
    upper_prev = send(upper7, [(7, 11)])
    z2 = pair((7,), True, got5, "again_end_lead")
    got6 = send(z2, [(7, 11)])
    got4_rest, solved = kernel_call(
        in_order, [narrow, wide], [got4_rest, solved], "upper_first", 10, aliases={0: 0, 1: 1}
    )
    upper11 = chained(
        functools.partial(steps_or_copy, 11, 7), [z2, *both, got3_last], "relax_last", 2
    )
    got6_rest = send(upper11, [(7, 9), (11, 15)])
    c9 = chained(
        functools.partial(steps_or_copy, 9, 11), [upper11, *both, got4_rest], "again_rest", 2
    )
    got5_rest = send(c9, [(9, 11), (11, 13)])
    base = chained(coarse_base, [upper_prev, own_w], "coarse_base", 1, wide)
    base = chained(lead_base, [base, own_w, got6], "lead_base", 2, wide)
    z3 = chained(again_end, [*both, base, got3, got4, z2, got5_rest], "again_end_rest", 2)
    got7 = send(z3, [(11, 13), (13, 15)])
    got7b = send(z3, [(11, 15), (3, 2), (5, 4), (7, 8)])
    c13 = chained(lead_two_steps, [z3, got5, *both, got6_rest, got7], "final_lead", 2)
    got8 = send(c13, [(13, 15), (9, 11)])
    got8b = send(c13, [(13, 14), (9, 10), (11, 12), (7, 6)])
    (solved,) = kernel_call(
        end_step, [wide], [got6_rest, *both, got7, got7b, solved], "coarse_end", 4, aliases={7: 0}
    )
    return kernel_call(
        last_sweep,
        [jax.ShapeDtypeStruct((COARSEN, CHANS, CELLS), F32)],
        [start, got8b, got8, got3, got4, got5, got6_rest, got7, got7b, *both, rhs_of_even, later_w, solved],
        "last_sweep",
        4,
        scratch=[
            pltpu.VMEM(STATE, F32),
            pltpu.VMEM((COARSEN, CHANS, CELLS), F32),
            pltpu.SemaphoreType.DMA((COARSEN,)),
        ],
    )[0]


def solution(mesh):
    return jax.shard_map(
        per_device,
        mesh=mesh,
        in_specs=(P(None, "batch"), P("layer", None, "batch"), P("layer", None, None)),
        out_specs=P("layer", None, "batch"),
        check_vma=False,
    )
```

```python
import functools

import jax
import jax.numpy as jnp
from jax import lax
from jax.experimental import pallas as pl
from jax.experimental.pallas import tpu as pltpu
from jax.sharding import PartitionSpec as P

SIDE = 16
CELLS = 256
CHANS = 256
TAPS = 9 * CHANS
COARSEN = 4
DEVICES = 16
F32 = jnp.float32
BF16 = jnp.bfloat16
STATE = (CELLS, CHANS)
VMEM_LIMIT = 12 << 20


def conv_tanh(state, weight):
    column = lax.broadcasted_iota(jnp.int32, STATE, 0) % SIDE
    before = jnp.where(column == 0, 0.0, pltpu.roll(state, 1, 0)).astype(BF16)
    after = jnp.where(column == SIDE - 1, 0.0, pltpu.roll(state, CELLS - 1, 0)).astype(BF16)
    here = state.astype(BF16)
    edge = jnp.zeros((SIDE, CHANS), BF16)

    def product(piece, row, column):
        if row == 0:
            piece = jnp.concatenate([edge, piece[:-SIDE]], 0)
        if row == 2:
            piece = jnp.concatenate([piece[SIDE:], edge], 0)
        tap = 3 * row + column
        return lax.dot_general(
            piece,
            weight[:, tap * CHANS : (tap + 1) * CHANS],
            (((1,), (1,)), ((), ())),
            preferred_element_type=F32,
        )

    total = product(here, 1, 1)
    for column, piece in ((1, -here), (0, -before), (2, -after)):
        for row in (0, 2) if column == 1 else (1, 0, 2):
            total = total - product(piece, row, column)
    return jnp.tanh(total)


def vmem(shape, dtype):
    return pltpu.VMEM(shape, dtype)


def kernel_call(body, outs, args, name, steps, hbm=(), scratch=(), aliases=None):
    def space(i):
        return pltpu.HBM if i in hbm else pltpu.VMEM

    args = [pltpu.with_memory_space_constraint(a, space(i)) for i, a in enumerate(args)]
    return pl.pallas_call(
        body,
        out_shape=outs,
        in_specs=[pl.BlockSpec(memory_space=space(i)) for i in range(len(args))],
        out_specs=[
            pl.BlockSpec(memory_space=pltpu.VMEM if hasattr(o, "memory_space") else pl.ANY)
            for o in outs
        ],
        scratch_shapes=list(scratch),
        input_output_aliases=aliases or {},
        compiler_params=pltpu.CompilerParams(vmem_limit_bytes=VMEM_LIMIT),
        cost_estimate=pl.CostEstimate(
            flops=steps * 2 * TAPS * CELLS * CHANS, bytes_accessed=1 << 20, transcendentals=0
        ),
        name=name,
    )(*args)


def place():
    return lax.axis_index("layer")


def first_sweep(first, *refs):
    inputs, guess, weights = refs[:3]
    cpoint, own_w, later_w, start, raw, sems = refs[-6:]
    me = place()

    early = (me % 2 == 1) | (me == 0)

    @pl.when(early if first else jnp.logical_not(early))
    def _():
        source = [pltpu.make_async_copy(weights.at[0], own_w, sems.at[1])]
        for i in range(COARSEN - 1):
            source.append(pltpu.make_async_copy(weights.at[i + 1], later_w.at[i], sems.at[i + 2]))
        begin = pltpu.make_async_copy(inputs, raw, sems.at[0])
        other = pltpu.make_async_copy(guess.at[0], raw, sems.at[0])

        @pl.when(me == 0)
        def _():
            begin.start()

        @pl.when(me > 0)
        def _():
            other.start()

        for copy in source:
            copy.start()
        other.wait()
        state = raw[...].T

        @pl.when(me == 0)
        def _():
            start[...] = state

        for i in range(COARSEN):
            source[i].wait()
            state = state + 0.25 * conv_tanh(state, own_w if i == 0 else later_w[i - 1])
        cpoint[...] = state.astype(BF16)

    if not first:

        @pl.when(me == 0)
        def _():
            cpoint[...] = refs[6][...]


def sweep(state, own_w, later_w, rhs):
    terms = []
    for i in range(COARSEN):
        terms.append(conv_tanh(state, own_w if i == 0 else later_w[i - 1]))
        state = state + 0.25 * terms[-1]
    rhs[...] = 0.25 * (terms[0] + terms[1] + terms[2] + terms[3]) - terms[0]
    return state


def second_sweep_lead(left_odd, own_w, later_w, _, rhs, solved, out):
    @pl.when(place() == 1)
    def _():
        out[...] = sweep(left_odd[...].astype(F32), own_w, later_w, rhs).astype(BF16)


def second_sweep_even(left_even, own_w, later_w, inputs, _, __, rhs, first, start, solved, raw, sem):
    me = place()

    @pl.when(me % 2 == 0)
    def _():
        left = jnp.where(me == 0, start[...], left_even[...].astype(F32))
        first[...] = sweep(left, own_w, later_w, rhs)

    @pl.when(me == 1)
    def _():
        copy = pltpu.make_async_copy(inputs, raw, sem)
        copy.start()
        copy.wait()
        start[...] = raw[...].T


def second_sweep_odd(left_odd, own_w, later_w, _, __, rhs, solved):
    me = place()

    @pl.when((me % 2 == 1) & (me > 1))
    def _():
        sweep(left_odd[...].astype(F32), own_w, later_w, rhs)


def in_order(*refs):
    pass


def either(me, owners):
    chosen = me == owners[0]
    for owner in owners[1:]:
        chosen |= me == owner
    return chosen


def both_steps(even_rhs, rhs, even_w, own_w, got):
    value = got[...].astype(F32)
    value = value + conv_tanh(value, even_w) + even_rhs[...]
    return value + conv_tanh(value, own_w) + rhs[...]


def two_steps(owners, keep, even_rhs, rhs, even_w, own_w, got, _, out, solved):
    @pl.when(either(place(), owners))
    def _():
        value = both_steps(even_rhs, rhs, even_w, own_w, got)
        if keep:
            solved[...] = value
        out[...] = value.astype(BF16)


def lead_half(got, even_w, _, out, solved):
    @pl.when(place() == 3)
    def _():
        value = got[...].astype(F32)
        out[...] = value + conv_tanh(value, even_w)


def lead_rest(rhs, own_w, even_rhs, part, _, out, solved):
    @pl.when(place() == 3)
    def _():
        value = part[...] + even_rhs[...]
        value = value + conv_tanh(value, own_w) + rhs[...]
        solved[...] = value
        out[...] = value.astype(BF16)

    @pl.when(place() == 7)
    def _():
        out[...] = rhs[...].astype(BF16)


def one_step(owners, first, rhs, own_w, _, out, solved):
    @pl.when(either(place(), owners))
    def _():
        value = first[...]
        out[...] = (value + conv_tanh(value, own_w) + rhs[...]).astype(BF16)


def coarse_step(got, own_w):
    value = got[...].astype(F32)
    return value + 4.0 * conv_tanh(value, own_w)


def relax_rest(rhs, own_w, odd_w, odd_rhs, got, _, out, solved):
    @pl.when(place() == 6)
    def _():
        value = got[...].astype(F32)
        value = value + conv_tanh(value, own_w) + rhs[...]
        value = value + conv_tanh(value, odd_w) + odd_rhs[...].astype(F32)
        out[...] = value.astype(BF16)


def steps_or_copy(owner, copier, other, even_rhs, rhs, even_w, own_w, got, _, out, solved):
    two_steps((owner,), False, even_rhs, rhs, even_w, own_w, got, _, out, solved)

    @pl.when(place() == copier)
    def _():
        out[...] = other[...]


def coarse_base(upper, own_w, _, out, solved):
    @pl.when(place() == 11)
    def _():
        out[...] = coarse_step(upper, own_w)


def lead_base(base, own_w, lead, _, out, solved):
    @pl.when(place() == 11)
    def _():
        out[...] = coarse_step(lead, own_w) - base[...]


def again_end(even_rhs, rhs, even_w, own_w, base, early3, early4, mine, got, _, out, solved):
    me = place()

    @pl.when(either(me, (11, 13)))
    def _():
        value = both_steps(even_rhs, rhs, even_w, own_w, got)
        value = value + jnp.where(me == 11, base[...], 0.0)
        solved[...] = value
        out[...] = value.astype(BF16)

    for owner, source in ((3, early3), (5, early4), (7, mine)):

        @pl.when(me == owner)
        def _():
            out[...] = source[...]


def lead_two_steps(mine, early5, even_rhs, rhs, even_w, own_w, rest, got, _, out, solved):
    two_steps((9,), False, even_rhs, rhs, even_w, own_w, rest, _, out, solved)
    two_steps((13,), False, even_rhs, rhs, even_w, own_w, got, _, out, solved)
    for owner, source in ((11, mine), (7, early5)):

        @pl.when(place() == owner)
        def _():
            out[...] = source[...]


def end_step(upper, even_rhs, rhs, even_w, own_w, got, lead, _, solved):
    @pl.when(place() == 15)
    def _():
        value = both_steps(even_rhs, rhs, even_w, own_w, got) - coarse_step(upper, own_w)
        solved[...] = value + coarse_step(lead, own_w)


def last_sweep(
    start, got8b, got8, got3, got4, got5, got6, got7, got7b,
    even_rhs, rhs, even_w, own_w, rhs_of_even, later_w, solved, states, left, ready, sems,
):
    me = place()
    sources = (
        (start, (0, 1)),
        (got7b, (2, 4, 8)),
        (got8b, (6, 10, 12, 14)),
        (got3, (3,)),
        (got4, (5,)),
        (got5, (7,)),
        (got6, (9,)),
        (got7, (13,)),
        (got8, (11, 15)),
    )
    for source, owners in sources:

        @pl.when(either(me, owners))
        def _():
            left[...] = source[...].astype(F32)

    @pl.when(me % 2 == 1)
    def _():
        value = left[...]
        left[...] = value + conv_tanh(value, even_w) + even_rhs[...]

    def store(i, value):
        ready[i] = value.T
        copy = pltpu.make_async_copy(ready.at[i], states.at[i], sems.at[i])
        copy.start()
        return copy

    state = left[...]
    term = conv_tanh(state, own_w)
    own = jnp.where(me % 2 == 0, rhs_of_even[...], rhs[...])
    end = jnp.where(me % 4 == 3, solved[...], state + term + own)
    copies = [store(COARSEN - 1, end)]
    state = state + 0.25 * term
    copies.append(store(0, state))
    for i in range(1, COARSEN - 1):
        state = state + 0.25 * conv_tanh(state, later_w[i - 1])
        copies.append(store(i, state))
    for copy in copies:
        copy.wait()


def per_device(inputs, guess, weights):
    def send(value, pairs):
        return lax.ppermute(value, "layer", pairs)

    narrow = vmem(STATE, BF16)
    wide = vmem(STATE, F32)
    held = [vmem((CHANS, TAPS), BF16), vmem((COARSEN - 1, CHANS, TAPS), BF16), wide]
    up_inside = [(i, i + 1) for i in range(0, DEVICES, 2)]
    up_between = [(i, i + 1) for i in range(1, DEVICES - 1, 2)]
    scratch = [pltpu.VMEM((CHANS, CELLS), F32), pltpu.SemaphoreType.DMA((COARSEN + 1,))]

    from_odd, *kept = kernel_call(
        functools.partial(first_sweep, True),
        [narrow, *held],
        [inputs, guess, weights],
        "first_sweep_odd",
        4,
        hbm=(0, 1, 2),
        scratch=scratch,
    )
    left_even = send(from_odd, up_between)
    from_even, own_w, later_w, start = kernel_call(
        functools.partial(first_sweep, False),
        [narrow, *held],
        [inputs, guess, weights, *kept, from_odd],
        "first_sweep_even",
        4,
        hbm=(0, 1, 2),
        scratch=scratch,
        aliases={3: 1, 4: 2, 5: 3},
    )
    left_odd = send(from_even, up_inside)
    even_w = send(own_w, [*up_inside, (7, 6)])

    left_even, start = kernel_call(
        in_order, [narrow, wide], [left_even, start], "even_first", 1, aliases={0: 0, 1: 1}
    )
    rhs, solved, c1 = kernel_call(
        second_sweep_lead,
        [wide, wide, narrow],
        [left_odd, own_w, later_w, start],
        "second_sweep_lead",
        40,
    )
    got3 = send(c1, [(1, 3)])
    rhs_of_even, first, start, solved = kernel_call(
        second_sweep_even,
        [wide, wide, wide, wide],
        [left_even, own_w, later_w, inputs, start, solved],
        "second_sweep_even",
        4,
        hbm=(3,),
        scratch=[pltpu.VMEM((CHANS, CELLS), F32), pltpu.SemaphoreType.DMA(())],
        aliases={4: 2, 5: 3},
    )
    even_rhs = send(rhs_of_even, up_inside)
    first = send(first, [(4, 5), (8, 9)])
    rhs, solved = kernel_call(
        second_sweep_odd,
        [wide, wide],
        [left_odd, own_w, later_w, rhs, solved],
        "second_sweep_odd",
        0,
        aliases={3: 0, 4: 1},
    )
    both = [even_rhs, rhs, even_w, own_w]

    def chained(body, args, name, steps, out=narrow):
        nonlocal solved
        value, solved = kernel_call(
            body, [out, wide], [*args, solved], name, steps, aliases={len(args): 1}
        )
        return value

    def pair(owners, keep, got, name):
        return chained(functools.partial(two_steps, owners, keep), [*both, got], name, 2)

    part = chained(lead_half, [got3, even_w], "lead_first", 7, wide)
    upper1 = chained(lead_rest, [rhs, own_w, even_rhs, part], "relax_lead", 20)
    got4 = send(upper1, [(3, 5), (7, 6)])
    c5 = chained(functools.partial(one_step, (5, 9)), [first, rhs, own_w], "relax_first", 1)
    got3_rest = send(c5, [(5, 6)])
    got3_last = send(c5, [(9, 11)])
    c5_lead = pair((5,), False, got4, "again_lead")
    got5 = send(c5_lead, [(5, 7)])
    upper6 = chained(
        relax_rest, [rhs_of_even, own_w, even_w, got4, got3_rest], "relax_rest", 2
    )
    got4_rest = send(upper6, [(6, 9)])
    upper_prev = send(upper6, [(6, 11)])
    z2 = pair((7,), True, got5, "again_end_lead")
    got6 = send(z2, [(7, 11)])
    got4_rest, solved = kernel_call(
        in_order, [narrow, wide], [got4_rest, solved], "upper_first", 10, aliases={0: 0, 1: 1}
    )
    upper11 = chained(
        functools.partial(steps_or_copy, 11, 7), [z2, *both, got3_last], "relax_last", 2
    )
    got6_rest = send(upper11, [(7, 9), (11, 15)])
    c9 = chained(
        functools.partial(steps_or_copy, 9, 11), [upper11, *both, got4_rest], "again_rest", 2
    )
    got5_rest = send(c9, [(9, 11), (11, 13)])
    base = chained(coarse_base, [upper_prev, own_w], "coarse_base", 1, wide)
    base = chained(lead_base, [base, own_w, got6], "lead_base", 2, wide)
    z3 = chained(again_end, [*both, base, got3, got4, z2, got5_rest], "again_end_rest", 2)
    got7 = send(z3, [(11, 13), (13, 15)])
    got7b = send(z3, [(11, 15), (3, 2), (5, 4), (7, 8)])
    c13 = chained(lead_two_steps, [z3, got5, *both, got6_rest, got7], "final_lead", 2)
    got8 = send(c13, [(13, 15), (9, 11)])
    got8b = send(c13, [(13, 14), (9, 10), (11, 12), (7, 6)])
    (solved,) = kernel_call(
        end_step, [wide], [got6_rest, *both, got7, got7b, solved], "coarse_end", 4, aliases={7: 0}
    )
    return kernel_call(
        last_sweep,
        [jax.ShapeDtypeStruct((COARSEN, CHANS, CELLS), F32)],
        [start, got8b, got8, got3, got4, got5, got6_rest, got7, got7b, *both, rhs_of_even, later_w, solved],
        "last_sweep",
        4,
        scratch=[
            pltpu.VMEM(STATE, F32),
            pltpu.VMEM((COARSEN, CHANS, CELLS), F32),
            pltpu.SemaphoreType.DMA((COARSEN,)),
        ],
    )[0]


def solution(mesh):
    return jax.shard_map(
        per_device,
        mesh=mesh,
        in_specs=(P(None, "batch"), P("layer", None, "batch"), P("layer", None, None)),
        out_specs=P("layer", None, "batch"),
        check_vma=False,
    )
```

```python
import functools

import jax
import jax.numpy as jnp
from jax import lax
from jax.experimental import pallas as pl
from jax.experimental.pallas import tpu as pltpu
from jax.sharding import PartitionSpec as P

SIDE = 16
CELLS = 256
CHANS = 256
TAPS = 9 * CHANS
COARSEN = 4
DEVICES = 16
F32 = jnp.float32
BF16 = jnp.bfloat16
STATE = (CELLS, CHANS)
VMEM_LIMIT = 12 << 20


def conv_tanh(state, weight):
    column = lax.broadcasted_iota(jnp.int32, STATE, 0) % SIDE
    before = jnp.where(column == 0, 0.0, pltpu.roll(state, 1, 0)).astype(BF16)
    after = jnp.where(column == SIDE - 1, 0.0, pltpu.roll(state, CELLS - 1, 0)).astype(BF16)
    here = state.astype(BF16)
    edge = jnp.zeros((SIDE, CHANS), BF16)

    def product(piece, row, column):
        if row == 0:
            piece = jnp.concatenate([edge, piece[:-SIDE]], 0)
        if row == 2:
            piece = jnp.concatenate([piece[SIDE:], edge], 0)
        tap = 3 * row + column
        return lax.dot_general(
            piece,
            weight[:, tap * CHANS : (tap + 1) * CHANS],
            (((1,), (1,)), ((), ())),
            preferred_element_type=F32,
        )

    total = product(here, 1, 1)
    for column, piece in ((1, -here), (0, -before), (2, -after)):
        for row in (0, 2) if column == 1 else (1, 0, 2):
            total = total - product(piece, row, column)
    return jnp.tanh(total)


def vmem(shape, dtype):
    return pltpu.VMEM(shape, dtype)


def kernel_call(body, outs, args, name, steps, hbm=(), scratch=(), aliases=None):
    def space(i):
        return pltpu.HBM if i in hbm else pltpu.VMEM

    args = [pltpu.with_memory_space_constraint(a, space(i)) for i, a in enumerate(args)]
    return pl.pallas_call(
        body,
        out_shape=outs,
        in_specs=[pl.BlockSpec(memory_space=space(i)) for i in range(len(args))],
        out_specs=[
            pl.BlockSpec(memory_space=pltpu.VMEM if hasattr(o, "memory_space") else pl.ANY)
            for o in outs
        ],
        scratch_shapes=list(scratch),
        input_output_aliases=aliases or {},
        compiler_params=pltpu.CompilerParams(vmem_limit_bytes=VMEM_LIMIT),
        cost_estimate=pl.CostEstimate(
            flops=steps * 2 * TAPS * CELLS * CHANS, bytes_accessed=1 << 20, transcendentals=0
        ),
        name=name,
    )(*args)


def place():
    return lax.axis_index("layer")


def first_sweep(first, *refs):
    inputs, guess, weights = refs[:3]
    cpoint, own_w, later_w, start, raw, sems = refs[-6:]
    me = place()

    early = (me % 2 == 1) | (me == 0)

    @pl.when(early if first else jnp.logical_not(early))
    def _():
        source = [pltpu.make_async_copy(weights.at[0], own_w, sems.at[1])]
        for i in range(COARSEN - 1):
            source.append(pltpu.make_async_copy(weights.at[i + 1], later_w.at[i], sems.at[i + 2]))
        begin = pltpu.make_async_copy(inputs, raw, sems.at[0])
        other = pltpu.make_async_copy(guess.at[0], raw, sems.at[0])

        @pl.when(me == 0)
        def _():
            begin.start()

        @pl.when(me > 0)
        def _():
            other.start()

        for copy in source:
            copy.start()
        other.wait()
        state = raw[...].T

        @pl.when(me == 0)
        def _():
            start[...] = state

        for i in range(COARSEN):
            source[i].wait()
            state = state + 0.25 * conv_tanh(state, own_w if i == 0 else later_w[i - 1])
        cpoint[...] = state.astype(BF16)

    if not first:

        @pl.when(me == 0)
        def _():
            cpoint[...] = refs[6][...]


def sweep(state, own_w, later_w, rhs):
    terms = []
    for i in range(COARSEN):
        terms.append(conv_tanh(state, own_w if i == 0 else later_w[i - 1]))
        state = state + 0.25 * terms[-1]
    rhs[...] = 0.25 * (terms[0] + terms[1] + terms[2] + terms[3]) - terms[0]
    return state


def second_sweep_lead(left_odd, own_w, later_w, _, rhs, solved, out):
    @pl.when(place() == 1)
    def _():
        out[...] = sweep(left_odd[...].astype(F32), own_w, later_w, rhs).astype(BF16)


def second_sweep_even(left_even, own_w, later_w, inputs, _, __, rhs, first, start, solved, sent, raw, sem):
    me = place()

    @pl.when(me % 2 == 0)
    def _():
        left = jnp.where(me == 0, start[...], left_even[...].astype(F32))
        first[...] = sweep(left, own_w, later_w, rhs)
        sent[...] = rhs[...].astype(BF16)

    @pl.when(me == 1)
    def _():
        copy = pltpu.make_async_copy(inputs, raw, sem)
        copy.start()
        copy.wait()
        start[...] = raw[...].T


def second_sweep_odd(left_odd, own_w, later_w, _, __, rhs, solved):
    me = place()

    @pl.when((me % 2 == 1) & (me > 1))
    def _():
        sweep(left_odd[...].astype(F32), own_w, later_w, rhs)


def in_order(*refs):
    pass


def either(me, owners):
    chosen = me == owners[0]
    for owner in owners[1:]:
        chosen |= me == owner
    return chosen


def both_steps(even_rhs, rhs, even_w, own_w, got):
    value = got[...].astype(F32)
    value = value + conv_tanh(value, even_w) + even_rhs[...].astype(F32)
    return value + conv_tanh(value, own_w) + rhs[...]


def two_steps(owners, keep, even_rhs, rhs, even_w, own_w, got, _, out, solved):
    @pl.when(either(place(), owners))
    def _():
        value = both_steps(even_rhs, rhs, even_w, own_w, got)
        if keep:
            solved[...] = value
        out[...] = value.astype(BF16)


def lead_half(got, even_w, _, out, solved):
    @pl.when(place() == 3)
    def _():
        value = got[...].astype(F32)
        out[...] = value + conv_tanh(value, even_w)


def lead_rest(rhs, own_w, even_rhs, part, _, out, solved):
    @pl.when(place() == 3)
    def _():
        value = part[...] + even_rhs[...].astype(F32)
        value = value + conv_tanh(value, own_w) + rhs[...]
        solved[...] = value
        out[...] = value.astype(BF16)


def one_step(owners, first, rhs, own_w, _, out, solved):
    @pl.when(either(place(), owners))
    def _():
        value = first[...]
        out[...] = (value + conv_tanh(value, own_w) + rhs[...]).astype(BF16)


def coarse_step(got, own_w):
    value = got[...].astype(F32)
    return value + 4.0 * conv_tanh(value, own_w)


def steps_or_copy(owner, copier, other, even_rhs, rhs, even_w, own_w, got, _, out, solved):
    two_steps((owner,), False, even_rhs, rhs, even_w, own_w, got, _, out, solved)

    @pl.when(place() == copier)
    def _():
        out[...] = other[...]


def coarse_base(upper, own_w, _, out, solved):
    @pl.when(place() == 11)
    def _():
        out[...] = coarse_step(upper, own_w)


def lead_base(base, own_w, lead, _, out, solved):
    @pl.when(place() == 11)
    def _():
        out[...] = coarse_step(lead, own_w) - base[...]


def again_end(even_rhs, rhs, even_w, own_w, base, early3, early4, mine, got, _, out, solved):
    me = place()

    @pl.when(either(me, (11, 13)))
    def _():
        value = both_steps(even_rhs, rhs, even_w, own_w, got)
        value = value + jnp.where(me == 11, base[...], 0.0)
        solved[...] = value
        out[...] = value.astype(BF16)

    for owner, source in ((3, early3), (5, early4), (7, mine)):

        @pl.when(me == owner)
        def _():
            out[...] = source[...]


def lead_two_steps(mine, early5, even_rhs, rhs, even_w, own_w, rest, got, _, out, solved):
    two_steps((9,), False, even_rhs, rhs, even_w, own_w, rest, _, out, solved)
    two_steps((13,), False, even_rhs, rhs, even_w, own_w, got, _, out, solved)
    for owner, source in ((11, mine), (7, early5)):

        @pl.when(place() == owner)
        def _():
            out[...] = source[...]


def end_step(upper, even_rhs, rhs, even_w, own_w, got, lead, _, solved):
    @pl.when(place() == 15)
    def _():
        value = both_steps(even_rhs, rhs, even_w, own_w, got) - coarse_step(upper, own_w)
        solved[...] = value + coarse_step(lead, own_w)


def last_sweep(
    start, got8b, got8, got3, got4, got5, got6, got7, got7b,
    even_rhs, rhs, even_w, own_w, rhs_of_even, later_w, solved, states, left, ready, sems,
):
    me = place()
    sources = (
        (start, (0, 1)),
        (got7b, (2, 4, 8)),
        (got8b, (6, 10, 12, 14)),
        (got3, (3,)),
        (got4, (5,)),
        (got5, (7,)),
        (got6, (9,)),
        (got7, (13,)),
        (got8, (11, 15)),
    )
    for source, owners in sources:

        @pl.when(either(me, owners))
        def _():
            left[...] = source[...].astype(F32)

    @pl.when(me % 2 == 1)
    def _():
        value = left[...]
        left[...] = value + conv_tanh(value, even_w) + even_rhs[...].astype(F32)

    def store(i, value):
        ready[i] = value.T
        copy = pltpu.make_async_copy(ready.at[i], states.at[i], sems.at[i])
        copy.start()
        return copy

    state = left[...]
    term = conv_tanh(state, own_w)
    own = jnp.where(me % 2 == 0, rhs_of_even[...], rhs[...])
    end = jnp.where(me % 4 == 3, solved[...], state + term + own)
    copies = [store(COARSEN - 1, end)]
    state = state + 0.25 * term
    copies.append(store(0, state))
    for i in range(1, COARSEN - 1):
        state = state + 0.25 * conv_tanh(state, later_w[i - 1])
        copies.append(store(i, state))
    for copy in copies:
        copy.wait()


def per_device(inputs, guess, weights):
    def send(value, pairs):
        return lax.ppermute(value, "layer", pairs)

    narrow = vmem(STATE, BF16)
    wide = vmem(STATE, F32)
    held = [vmem((CHANS, TAPS), BF16), vmem((COARSEN - 1, CHANS, TAPS), BF16), wide]
    up_inside = [(i, i + 1) for i in range(0, DEVICES, 2)]
    up_between = [(i, i + 1) for i in range(1, DEVICES - 1, 2)]
    scratch = [pltpu.VMEM((CHANS, CELLS), F32), pltpu.SemaphoreType.DMA((COARSEN + 1,))]

    from_odd, *kept = kernel_call(
        functools.partial(first_sweep, True),
        [narrow, *held],
        [inputs, guess, weights],
        "first_sweep_odd",
        4,
        hbm=(0, 1, 2),
        scratch=scratch,
    )
    left_even = send(from_odd, up_between)
    from_even, own_w, later_w, start = kernel_call(
        functools.partial(first_sweep, False),
        [narrow, *held],
        [inputs, guess, weights, *kept, from_odd],
        "first_sweep_even",
        4,
        hbm=(0, 1, 2),
        scratch=scratch,
        aliases={3: 1, 4: 2, 5: 3},
    )
    left_odd = send(from_even, up_inside)
    even_w = send(own_w, up_inside)

    left_even, start = kernel_call(
        in_order, [narrow, wide], [left_even, start], "even_first", 1, aliases={0: 0, 1: 1}
    )
    rhs, solved, c1 = kernel_call(
        second_sweep_lead,
        [wide, wide, narrow],
        [left_odd, own_w, later_w, start],
        "second_sweep_lead",
        40,
    )
    got3 = send(c1, [(1, 3)])
    rhs_of_even, first, start, solved, sent = kernel_call(
        second_sweep_even,
        [wide, wide, wide, wide, narrow],
        [left_even, own_w, later_w, inputs, start, solved],
        "second_sweep_even",
        4,
        hbm=(3,),
        scratch=[pltpu.VMEM((CHANS, CELLS), F32), pltpu.SemaphoreType.DMA(())],
        aliases={4: 2, 5: 3},
    )
    even_rhs = send(sent, up_inside)
    first = send(first, [(4, 5), (8, 9)])
    rhs, solved = kernel_call(
        second_sweep_odd,
        [wide, wide],
        [left_odd, own_w, later_w, rhs, solved],
        "second_sweep_odd",
        0,
        aliases={3: 0, 4: 1},
    )
    both = [even_rhs, rhs, even_w, own_w]

    def chained(body, args, name, steps, out=narrow):
        nonlocal solved
        value, solved = kernel_call(
            body, [out, wide], [*args, solved], name, steps, aliases={len(args): 1}
        )
        return value

    def pair(owners, keep, got, name):
        return chained(functools.partial(two_steps, owners, keep), [*both, got], name, 2)

    part = chained(lead_half, [got3, even_w], "lead_first", 7, wide)
    upper1 = chained(lead_rest, [rhs, own_w, even_rhs, part], "relax_lead", 20)
    got4 = send(upper1, [(3, 5)])
    c5 = chained(functools.partial(one_step, (5, 9)), [first, rhs, own_w], "relax_first", 1)
    got3_rest = send(c5, [(5, 7)])
    got3_last = send(c5, [(9, 11)])
    c5_lead = pair((5,), False, got4, "again_lead")
    got5 = send(c5_lead, [(5, 7)])
    upper7 = pair((7,), False, got3_rest, "relax_rest")
    got4_rest = send(upper7, [(7, 9)])
    upper_prev = send(upper7, [(7, 11)])
    z2 = pair((7,), True, got5, "again_end_lead")
    got6 = send(z2, [(7, 11)])
    got4_rest, solved = kernel_call(
        in_order, [narrow, wide], [got4_rest, solved], "upper_first", 10, aliases={0: 0, 1: 1}
    )
    upper11 = chained(
        functools.partial(steps_or_copy, 11, 7), [z2, *both, got3_last], "relax_last", 2
    )
    got6_rest = send(upper11, [(7, 9), (11, 15)])
    c9 = chained(
        functools.partial(steps_or_copy, 9, 11), [upper11, *both, got4_rest], "again_rest", 2
    )
    got5_rest = send(c9, [(9, 11), (11, 13)])
    base = chained(coarse_base, [upper_prev, own_w], "coarse_base", 1, wide)
    base = chained(lead_base, [base, own_w, got6], "lead_base", 2, wide)
    z3 = chained(again_end, [*both, base, got3, got4, z2, got5_rest], "again_end_rest", 2)
    got7 = send(z3, [(11, 13), (13, 15)])
    got7b = send(z3, [(11, 15), (3, 2), (5, 4), (7, 8)])
    c13 = chained(lead_two_steps, [z3, got5, *both, got6_rest, got7], "final_lead", 2)
    got8 = send(c13, [(13, 15), (9, 11)])
    got8b = send(c13, [(13, 14), (9, 10), (11, 12), (7, 6)])
    (solved,) = kernel_call(
        end_step, [wide], [got6_rest, *both, got7, got7b, solved], "coarse_end", 4, aliases={7: 0}
    )
    return kernel_call(
        last_sweep,
        [jax.ShapeDtypeStruct((COARSEN, CHANS, CELLS), F32)],
        [start, got8b, got8, got3, got4, got5, got6_rest, got7, got7b, *both, rhs_of_even, later_w, solved],
        "last_sweep",
        4,
        scratch=[
            pltpu.VMEM(STATE, F32),
            pltpu.VMEM((COARSEN, CHANS, CELLS), F32),
            pltpu.SemaphoreType.DMA((COARSEN,)),
        ],
    )[0]


def solution(mesh):
    return jax.shard_map(
        per_device,
        mesh=mesh,
        in_specs=(P(None, "batch"), P("layer", None, "batch"), P("layer", None, None)),
        out_specs=P("layer", None, "batch"),
        check_vma=False,
    )
```

```python
import functools

import jax
import jax.numpy as jnp
from jax import lax
from jax.experimental import pallas as pl
from jax.experimental.pallas import tpu as pltpu
from jax.sharding import PartitionSpec as P

SIDE = 16
CELLS = 256
CHANS = 256
TAPS = 9 * CHANS
COARSEN = 4
DEVICES = 16
F32 = jnp.float32
BF16 = jnp.bfloat16
STATE = (CELLS, CHANS)
VMEM_LIMIT = 12 << 20


def conv_tanh(state, weight):
    column = lax.broadcasted_iota(jnp.int32, STATE, 0) % SIDE
    before = jnp.where(column == 0, 0.0, pltpu.roll(state, 1, 0)).astype(BF16)
    after = jnp.where(column == SIDE - 1, 0.0, pltpu.roll(state, CELLS - 1, 0)).astype(BF16)
    here = state.astype(BF16)
    edge = jnp.zeros((SIDE, CHANS), BF16)

    def product(piece, row, column):
        if row == 0:
            piece = jnp.concatenate([edge, piece[:-SIDE]], 0)
        if row == 2:
            piece = jnp.concatenate([piece[SIDE:], edge], 0)
        tap = 3 * row + column
        return lax.dot_general(
            piece,
            weight[:, tap * CHANS : (tap + 1) * CHANS],
            (((1,), (1,)), ((), ())),
            preferred_element_type=F32,
        )

    total = product(here, 1, 1)
    for column, piece in ((1, -here), (0, -before), (2, -after)):
        for row in (0, 2) if column == 1 else (1, 0, 2):
            total = total - product(piece, row, column)
    return jnp.tanh(total)


def vmem(shape, dtype):
    return pltpu.VMEM(shape, dtype)


def kernel_call(body, outs, args, name, steps, hbm=(), scratch=(), aliases=None):
    def space(i):
        return pltpu.HBM if i in hbm else pltpu.VMEM

    args = [pltpu.with_memory_space_constraint(a, space(i)) for i, a in enumerate(args)]
    return pl.pallas_call(
        body,
        out_shape=outs,
        in_specs=[pl.BlockSpec(memory_space=space(i)) for i in range(len(args))],
        out_specs=[
            pl.BlockSpec(memory_space=pltpu.VMEM if hasattr(o, "memory_space") else pl.ANY)
            for o in outs
        ],
        scratch_shapes=list(scratch),
        input_output_aliases=aliases or {},
        compiler_params=pltpu.CompilerParams(vmem_limit_bytes=VMEM_LIMIT),
        cost_estimate=pl.CostEstimate(
            flops=steps * 2 * TAPS * CELLS * CHANS, bytes_accessed=1 << 20, transcendentals=0
        ),
        name=name,
    )(*args)


def place():
    return lax.axis_index("layer")


def first_sweep(first, *refs):
    inputs, guess, weights = refs[:3]
    cpoint, own_w, later_w, start, raw, sems = refs[-6:]
    me = place()

    early = (me % 2 == 1) | (me == 0)

    @pl.when(early if first else jnp.logical_not(early))
    def _():
        source = [pltpu.make_async_copy(weights.at[0], own_w, sems.at[1])]
        for i in range(COARSEN - 1):
            source.append(pltpu.make_async_copy(weights.at[i + 1], later_w.at[i], sems.at[i + 2]))
        begin = pltpu.make_async_copy(inputs, raw, sems.at[0])
        other = pltpu.make_async_copy(guess.at[0], raw, sems.at[0])

        @pl.when(me == 0)
        def _():
            begin.start()

        @pl.when(me > 0)
        def _():
            other.start()

        for copy in source:
            copy.start()
        other.wait()
        state = raw[...].T

        @pl.when(me == 0)
        def _():
            start[...] = state

        for i in range(COARSEN):
            source[i].wait()
            state = state + 0.25 * conv_tanh(state, own_w if i == 0 else later_w[i - 1])
        cpoint[...] = state.astype(BF16)

    if not first:

        @pl.when(me == 0)
        def _():
            cpoint[...] = refs[6][...]


def sweep(state, own_w, later_w, rhs):
    terms = []
    for i in range(COARSEN):
        terms.append(conv_tanh(state, own_w if i == 0 else later_w[i - 1]))
        state = state + 0.25 * terms[-1]
    rhs[...] = 0.25 * (terms[0] + terms[1] + terms[2] + terms[3]) - terms[0]
    return state


def second_sweep_lead(left_odd, own_w, later_w, _, rhs, solved, out):
    @pl.when(place() == 1)
    def _():
        out[...] = sweep(left_odd[...].astype(F32), own_w, later_w, rhs).astype(BF16)


def second_sweep_even(left_even, own_w, later_w, inputs, _, __, rhs, first, start, solved, sent, raw, sem):
    me = place()

    @pl.when(me % 2 == 0)
    def _():
        left = jnp.where(me == 0, start[...], left_even[...].astype(F32))
        first[...] = sweep(left, own_w, later_w, rhs)
        sent[...] = rhs[...].astype(BF16)

    @pl.when(me == 1)
    def _():
        copy = pltpu.make_async_copy(inputs, raw, sem)
        copy.start()
        copy.wait()
        start[...] = raw[...].T


def second_sweep_odd(left_odd, own_w, later_w, _, __, rhs, solved):
    me = place()

    @pl.when((me % 2 == 1) & (me > 1))
    def _():
        sweep(left_odd[...].astype(F32), own_w, later_w, rhs)


def in_order(*refs):
    pass


def either(me, owners):
    chosen = me == owners[0]
    for owner in owners[1:]:
        chosen |= me == owner
    return chosen


def both_steps(even_rhs, rhs, even_w, own_w, got):
    value = got[...].astype(F32)
    value = value + conv_tanh(value, even_w) + even_rhs[...].astype(F32)
    return value + conv_tanh(value, own_w) + rhs[...]


def two_steps(owners, keep, even_rhs, rhs, even_w, own_w, got, _, out, solved):
    @pl.when(either(place(), owners))
    def _():
        value = both_steps(even_rhs, rhs, even_w, own_w, got)
        if keep:
            solved[...] = value
        out[...] = value.astype(BF16)


def lead_half(got, even_w, _, out, solved):
    @pl.when(place() == 3)
    def _():
        value = got[...].astype(F32)
        out[...] = value + conv_tanh(value, even_w)


def lead_rest(rhs, own_w, even_rhs, part, _, out, solved):
    @pl.when(place() == 3)
    def _():
        value = part[...] + even_rhs[...].astype(F32)
        value = value + conv_tanh(value, own_w) + rhs[...]
        solved[...] = value
        out[...] = value.astype(BF16)


def one_step(owners, first, rhs, own_w, _, out, solved):
    @pl.when(either(place(), owners))
    def _():
        value = first[...]
        out[...] = (value + conv_tanh(value, own_w) + rhs[...]).astype(BF16)


def coarse_step(got, own_w):
    value = got[...].astype(F32)
    return value + 4.0 * conv_tanh(value, own_w)


def steps_or_copy(owner, copier, other, even_rhs, rhs, even_w, own_w, got, _, out, solved):
    two_steps((owner,), False, even_rhs, rhs, even_w, own_w, got, _, out, solved)

    @pl.when(place() == copier)
    def _():
        out[...] = other[...]


def coarse_base(upper, own_w, _, out, solved):
    @pl.when(place() == 11)
    def _():
        out[...] = coarse_step(upper, own_w)


def lead_base(base, own_w, lead, _, out, solved):
    @pl.when(place() == 11)
    def _():
        out[...] = coarse_step(lead, own_w) - base[...]


def again_end(even_rhs, rhs, even_w, own_w, base, early3, early4, mine, got, _, out, solved):
    me = place()

    @pl.when(either(me, (11, 13)))
    def _():
        value = both_steps(even_rhs, rhs, even_w, own_w, got)
        value = value + jnp.where(me == 11, base[...], 0.0)
        solved[...] = value
        out[...] = value.astype(BF16)

    for owner, source in ((3, early3), (5, early4), (7, mine)):

        @pl.when(me == owner)
        def _():
            out[...] = source[...]


def lead_two_steps(mine, early5, even_rhs, rhs, even_w, own_w, rest, got, _, out, solved):
    two_steps((9,), False, even_rhs, rhs, even_w, own_w, rest, _, out, solved)
    two_steps((13,), False, even_rhs, rhs, even_w, own_w, got, _, out, solved)
    for owner, source in ((11, mine), (7, early5)):

        @pl.when(place() == owner)
        def _():
            out[...] = source[...]


def end_step(upper, even_rhs, rhs, even_w, own_w, got, lead, _, solved):
    @pl.when(place() == 15)
    def _():
        value = both_steps(even_rhs, rhs, even_w, own_w, got) - coarse_step(upper, own_w)
        solved[...] = value + coarse_step(lead, own_w)


def last_sweep(
    start, got8b, got8, got3, got4, got5, got6, got7, got7b,
    even_rhs, rhs, even_w, own_w, rhs_of_even, later_w, solved, states, left, ready, sems,
):
    me = place()
    sources = (
        (start, (0, 1)),
        (got7b, (2, 4, 8)),
        (got8b, (6, 10, 12, 14)),
        (got3, (3,)),
        (got4, (5,)),
        (got5, (7,)),
        (got6, (9,)),
        (got7, (13,)),
        (got8, (11, 15)),
    )
    for source, owners in sources:

        @pl.when(either(me, owners))
        def _():
            left[...] = source[...].astype(F32)

    @pl.when(me % 2 == 1)
    def _():
        value = left[...]
        left[...] = value + conv_tanh(value, even_w) + even_rhs[...].astype(F32)

    def store(i, value):
        ready[i] = value.T
        copy = pltpu.make_async_copy(ready.at[i], states.at[i], sems.at[i])
        copy.start()
        return copy

    state = left[...]
    term = conv_tanh(state, own_w)
    own = jnp.where(me % 2 == 0, rhs_of_even[...], rhs[...])
    end = jnp.where(me % 4 == 3, solved[...], state + term + own)
    copies = [store(COARSEN - 1, end)]
    state = state + 0.25 * term
    copies.append(store(0, state))
    for i in range(1, COARSEN - 1):
        state = state + 0.25 * conv_tanh(state, later_w[i - 1])
        copies.append(store(i, state))
    for copy in copies:
        copy.wait()


def per_device(inputs, guess, weights):
    def send(value, pairs):
        return lax.ppermute(value, "layer", pairs)

    narrow = vmem(STATE, BF16)
    wide = vmem(STATE, F32)
    held = [vmem((CHANS, TAPS), BF16), vmem((COARSEN - 1, CHANS, TAPS), BF16), wide]
    up_inside = [(i, i + 1) for i in range(0, DEVICES, 2)]
    up_between = [(i, i + 1) for i in range(1, DEVICES - 1, 2)]
    scratch = [pltpu.VMEM((CHANS, CELLS), F32), pltpu.SemaphoreType.DMA((COARSEN + 1,))]

    from_odd, *kept = kernel_call(
        functools.partial(first_sweep, True),
        [narrow, *held],
        [inputs, guess, weights],
        "first_sweep_odd",
        4,
        hbm=(0, 1, 2),
        scratch=scratch,
    )
    left_even = send(from_odd, up_between)
    from_even, own_w, later_w, start = kernel_call(
        functools.partial(first_sweep, False),
        [narrow, *held],
        [inputs, guess, weights, *kept, from_odd],
        "first_sweep_even",
        4,
        hbm=(0, 1, 2),
        scratch=scratch,
        aliases={3: 1, 4: 2, 5: 3},
    )
    left_odd = send(from_even, up_inside)
    even_w = send(own_w, up_inside)

    left_even, start = kernel_call(
        in_order, [narrow, wide], [left_even, start], "even_first", 1, aliases={0: 0, 1: 1}
    )
    rhs, solved, c1 = kernel_call(
        second_sweep_lead,
        [wide, wide, narrow],
        [left_odd, own_w, later_w, start],
        "second_sweep_lead",
        40,
    )
    got3 = send(c1, [(1, 3)])
    rhs_of_even, first, start, solved, sent = kernel_call(
        second_sweep_even,
        [wide, wide, wide, wide, narrow],
        [left_even, own_w, later_w, inputs, start, solved],
        "second_sweep_even",
        4,
        hbm=(3,),
        scratch=[pltpu.VMEM((CHANS, CELLS), F32), pltpu.SemaphoreType.DMA(())],
        aliases={4: 2, 5: 3},
    )
    even_rhs = send(sent, up_inside)
    first = send(first, [(4, 5), (8, 9)])
    rhs, solved = kernel_call(
        second_sweep_odd,
        [wide, wide],
        [left_odd, own_w, later_w, rhs, solved],
        "second_sweep_odd",
        0,
        aliases={3: 0, 4: 1},
    )
    both = [even_rhs, rhs, even_w, own_w]

    def chained(body, args, name, steps, out=narrow):
        nonlocal solved
        value, solved = kernel_call(
            body, [out, wide], [*args, solved], name, steps, aliases={len(args): 1}
        )
        return value

    def pair(owners, keep, got, name):
        return chained(functools.partial(two_steps, owners, keep), [*both, got], name, 2)

    part = chained(lead_half, [got3, even_w], "lead_first", 7, wide)
    upper1 = chained(lead_rest, [rhs, own_w, even_rhs, part], "relax_lead", 20)
    got4 = send(upper1, [(3, 5)])
    c5 = chained(functools.partial(one_step, (5, 9)), [first, rhs, own_w], "relax_first", 1)
    got3_rest = send(c5, [(5, 7)])
    got3_last = send(c5, [(9, 11)])
    c5_lead = pair((5,), False, got4, "again_lead")
    got5 = send(c5_lead, [(5, 7)])
    upper7 = pair((7,), False, got3_rest, "relax_rest")
    got4_rest = send(upper7, [(7, 9)])
    upper_prev = send(upper7, [(7, 11)])
    got3_last, solved = kernel_call(
        in_order, [narrow, wide], [got3_last, solved], "last_first", 1, aliases={0: 0, 1: 1}
    )
    z2 = pair((7,), True, got5, "again_end_lead")
    got6 = send(z2, [(7, 11)])
    got4_rest, solved = kernel_call(
        in_order, [narrow, wide], [got4_rest, solved], "upper_first", 10, aliases={0: 0, 1: 1}
    )
    upper11 = chained(
        functools.partial(steps_or_copy, 11, 7), [z2, *both, got3_last], "relax_last", 2
    )
    got6_rest = send(upper11, [(7, 9), (11, 15)])
    c9 = chained(
        functools.partial(steps_or_copy, 9, 11), [upper11, *both, got4_rest], "again_rest", 2
    )
    got5_rest = send(c9, [(9, 11), (11, 13)])
    base = chained(coarse_base, [upper_prev, own_w], "coarse_base", 1, wide)
    base = chained(lead_base, [base, own_w, got6], "lead_base", 2, wide)
    z3 = chained(again_end, [*both, base, got3, got4, z2, got5_rest], "again_end_rest", 2)
    got7 = send(z3, [(11, 13), (13, 15)])
    got7b = send(z3, [(11, 15), (3, 2), (5, 4), (7, 8)])
    c13 = chained(lead_two_steps, [z3, got5, *both, got6_rest, got7], "final_lead", 2)
    got8 = send(c13, [(13, 15), (9, 11)])
    got8b = send(c13, [(13, 14), (9, 10), (11, 12), (7, 6)])
    (solved,) = kernel_call(
        end_step, [wide], [got6_rest, *both, got7, got7b, solved], "coarse_end", 4, aliases={7: 0}
    )
    return kernel_call(
        last_sweep,
        [jax.ShapeDtypeStruct((COARSEN, CHANS, CELLS), F32)],
        [start, got8b, got8, got3, got4, got5, got6_rest, got7, got7b, *both, rhs_of_even, later_w, solved],
        "last_sweep",
        4,
        scratch=[
            pltpu.VMEM(STATE, F32),
            pltpu.VMEM((COARSEN, CHANS, CELLS), F32),
            pltpu.SemaphoreType.DMA((COARSEN,)),
        ],
    )[0]


def solution(mesh):
    return jax.shard_map(
        per_device,
        mesh=mesh,
        in_specs=(P(None, "batch"), P("layer", None, "batch"), P("layer", None, None)),
        out_specs=P("layer", None, "batch"),
        check_vma=False,
    )
```

```python
import functools

import jax
import jax.numpy as jnp
from jax import lax
from jax.experimental import pallas as pl
from jax.experimental.pallas import tpu as pltpu
from jax.sharding import PartitionSpec as P

SIDE = 16
CELLS = 256
CHANS = 256
TAPS = 9 * CHANS
COARSEN = 4
DEVICES = 16
F32 = jnp.float32
BF16 = jnp.bfloat16
STATE = (CELLS, CHANS)
VMEM_LIMIT = 12 << 20


def conv_tanh(state, weight):
    column = lax.broadcasted_iota(jnp.int32, STATE, 0) % SIDE
    before = jnp.where(column == 0, 0.0, pltpu.roll(state, 1, 0)).astype(BF16)
    after = jnp.where(column == SIDE - 1, 0.0, pltpu.roll(state, CELLS - 1, 0)).astype(BF16)
    here = state.astype(BF16)
    edge = jnp.zeros((SIDE, CHANS), BF16)

    def product(piece, row, column):
        if row == 0:
            piece = jnp.concatenate([edge, piece[:-SIDE]], 0)
        if row == 2:
            piece = jnp.concatenate([piece[SIDE:], edge], 0)
        tap = 3 * row + column
        return lax.dot_general(
            piece,
            weight[:, tap * CHANS : (tap + 1) * CHANS],
            (((1,), (1,)), ((), ())),
            preferred_element_type=F32,
        )

    total = product(here, 1, 1)
    for column, piece in ((1, -here), (0, -before), (2, -after)):
        for row in (0, 2) if column == 1 else (1, 0, 2):
            total = total - product(piece, row, column)
    return jnp.tanh(total)


def vmem(shape, dtype):
    return pltpu.VMEM(shape, dtype)


def kernel_call(body, outs, args, name, steps, hbm=(), scratch=(), aliases=None):
    def space(i):
        return pltpu.HBM if i in hbm else pltpu.VMEM

    args = [pltpu.with_memory_space_constraint(a, space(i)) for i, a in enumerate(args)]
    return pl.pallas_call(
        body,
        out_shape=outs,
        in_specs=[pl.BlockSpec(memory_space=space(i)) for i in range(len(args))],
        out_specs=[
            pl.BlockSpec(memory_space=pltpu.VMEM if hasattr(o, "memory_space") else pl.ANY)
            for o in outs
        ],
        scratch_shapes=list(scratch),
        input_output_aliases=aliases or {},
        compiler_params=pltpu.CompilerParams(vmem_limit_bytes=VMEM_LIMIT),
        cost_estimate=pl.CostEstimate(
            flops=steps * 2 * TAPS * CELLS * CHANS, bytes_accessed=1 << 20, transcendentals=0
        ),
        name=name,
    )(*args)


def place():
    return lax.axis_index("layer")


def first_sweep(first, *refs):
    inputs, guess, weights = refs[:3]
    cpoint, own_w, later_w, start, raw, sems = refs[-6:]
    me = place()

    early = (me % 2 == 1) | (me == 0)

    @pl.when(early if first else jnp.logical_not(early))
    def _():
        source = [pltpu.make_async_copy(weights.at[0], own_w, sems.at[1])]
        for i in range(COARSEN - 1):
            source.append(pltpu.make_async_copy(weights.at[i + 1], later_w.at[i], sems.at[i + 2]))
        begin = pltpu.make_async_copy(inputs, raw, sems.at[0])
        other = pltpu.make_async_copy(guess.at[0], raw, sems.at[0])

        @pl.when(me == 0)
        def _():
            begin.start()

        @pl.when(me > 0)
        def _():
            other.start()

        for copy in source:
            copy.start()
        other.wait()
        state = raw[...].T

        @pl.when(me == 0)
        def _():
            start[...] = state

        for i in range(COARSEN):
            source[i].wait()
            state = state + 0.25 * conv_tanh(state, own_w if i == 0 else later_w[i - 1])
        cpoint[...] = state.astype(BF16)

    if not first:

        @pl.when(me == 0)
        def _():
            cpoint[...] = refs[6][...]


def sweep(state, own_w, later_w, rhs):
    terms = []
    for i in range(COARSEN):
        terms.append(conv_tanh(state, own_w if i == 0 else later_w[i - 1]))
        state = state + 0.25 * terms[-1]
    rhs[...] = 0.25 * (terms[0] + terms[1] + terms[2] + terms[3]) - terms[0]
    return state


def second_sweep_lead(left_odd, own_w, later_w, _, rhs, solved, out):
    @pl.when(place() == 1)
    def _():
        out[...] = sweep(left_odd[...].astype(F32), own_w, later_w, rhs).astype(BF16)


def second_sweep_even(left_even, own_w, later_w, inputs, _, __, rhs, first, start, solved, sent, raw, sem):
    me = place()

    @pl.when(me % 2 == 0)
    def _():
        left = jnp.where(me == 0, start[...], left_even[...].astype(F32))
        first[...] = sweep(left, own_w, later_w, rhs)
        sent[...] = rhs[...].astype(BF16)

    @pl.when(me == 1)
    def _():
        copy = pltpu.make_async_copy(inputs, raw, sem)
        copy.start()
        copy.wait()
        start[...] = raw[...].T


def second_sweep_odd(left_odd, own_w, later_w, _, __, rhs, solved):
    me = place()

    @pl.when((me % 2 == 1) & (me > 1))
    def _():
        sweep(left_odd[...].astype(F32), own_w, later_w, rhs)


def in_order(*refs):
    pass


def either(me, owners):
    chosen = me == owners[0]
    for owner in owners[1:]:
        chosen |= me == owner
    return chosen


def both_steps(even_rhs, rhs, even_w, own_w, got):
    value = got[...].astype(F32)
    value = value + conv_tanh(value, even_w) + even_rhs[...].astype(F32)
    return value + conv_tanh(value, own_w) + rhs[...]


def two_steps(owners, keep, even_rhs, rhs, even_w, own_w, got, _, out, solved):
    @pl.when(either(place(), owners))
    def _():
        value = both_steps(even_rhs, rhs, even_w, own_w, got)
        if keep:
            solved[...] = value
        out[...] = value.astype(BF16)


def lead_half(got, even_w, _, out, solved):
    @pl.when(place() == 3)
    def _():
        value = got[...].astype(F32)
        out[...] = value + conv_tanh(value, even_w)


def lead_rest(rhs, own_w, even_rhs, part, _, out, solved):
    @pl.when(place() == 3)
    def _():
        value = part[...] + even_rhs[...].astype(F32)
        value = value + conv_tanh(value, own_w) + rhs[...]
        solved[...] = value
        out[...] = value.astype(BF16)


def one_step(owners, first, rhs, own_w, _, out, solved):
    @pl.when(either(place(), owners))
    def _():
        value = first[...]
        out[...] = (value + conv_tanh(value, own_w) + rhs[...]).astype(BF16)


def coarse_step(got, own_w):
    value = got[...].astype(F32)
    return value + 4.0 * conv_tanh(value, own_w)


def steps_or_copy(owner, copier, other, even_rhs, rhs, even_w, own_w, got, _, out, solved):
    two_steps((owner,), False, even_rhs, rhs, even_w, own_w, got, _, out, solved)

    @pl.when(place() == copier)
    def _():
        out[...] = other[...]


def coarse_base(upper, own_w, _, out, solved):
    @pl.when(place() == 11)
    def _():
        out[...] = coarse_step(upper, own_w)


def lead_base(base, own_w, lead, _, out, solved):
    @pl.when(place() == 11)
    def _():
        out[...] = coarse_step(lead, own_w) - base[...]


def again_end(even_rhs, rhs, even_w, own_w, base, early3, early4, mine, got, _, out, solved):
    me = place()

    @pl.when(either(me, (11, 13)))
    def _():
        value = both_steps(even_rhs, rhs, even_w, own_w, got)
        value = value + jnp.where(me == 11, base[...], 0.0)
        solved[...] = value
        out[...] = value.astype(BF16)

    for owner, source in ((3, early3), (5, early4), (7, mine)):

        @pl.when(me == owner)
        def _():
            out[...] = source[...]


def lead_two_steps(mine, early5, even_rhs, rhs, even_w, own_w, rest, got, _, out, solved):
    two_steps((9,), False, even_rhs, rhs, even_w, own_w, rest, _, out, solved)
    two_steps((13,), False, even_rhs, rhs, even_w, own_w, got, _, out, solved)
    for owner, source in ((11, mine), (7, early5)):

        @pl.when(place() == owner)
        def _():
            out[...] = source[...]


def end_step(upper, even_rhs, rhs, even_w, own_w, got, lead, _, solved):
    @pl.when(place() == 15)
    def _():
        value = both_steps(even_rhs, rhs, even_w, own_w, got) - coarse_step(upper, own_w)
        solved[...] = value + coarse_step(lead, own_w)


def last_sweep(
    start, got8b, got8, got3, got4, got5, got6, got7, got7b,
    even_rhs, rhs, even_w, own_w, rhs_of_even, later_w, solved, states, left, ready, sems,
):
    me = place()
    sources = (
        (start, (0, 1)),
        (got7b, (2, 4, 8)),
        (got8b, (6, 10, 12, 14)),
        (got3, (3,)),
        (got4, (5,)),
        (got5, (7,)),
        (got6, (9,)),
        (got7, (13,)),
        (got8, (11, 15)),
    )
    for source, owners in sources:

        @pl.when(either(me, owners))
        def _():
            left[...] = source[...].astype(F32)

    @pl.when(me % 2 == 1)
    def _():
        value = left[...]
        left[...] = value + conv_tanh(value, even_w) + even_rhs[...].astype(F32)

    def store(i, value):
        ready[i] = value.T
        copy = pltpu.make_async_copy(ready.at[i], states.at[i], sems.at[i])
        copy.start()
        return copy

    state = left[...]
    term = conv_tanh(state, own_w)
    own = jnp.where(me % 2 == 0, rhs_of_even[...], rhs[...])
    end = jnp.where(me % 4 == 3, solved[...], state + term + own)
    first = state + 0.25 * term
    middle = first + 0.25 * conv_tanh(first, later_w[0])
    copies = [store(COARSEN - 1, end), store(0, first), store(1, middle)]
    copies.append(store(2, middle + 0.25 * conv_tanh(middle, later_w[1])))
    for copy in copies:
        copy.wait()


def per_device(inputs, guess, weights):
    def send(value, pairs):
        return lax.ppermute(value, "layer", pairs)

    narrow = vmem(STATE, BF16)
    wide = vmem(STATE, F32)
    held = [vmem((CHANS, TAPS), BF16), vmem((COARSEN - 1, CHANS, TAPS), BF16), wide]
    up_inside = [(i, i + 1) for i in range(0, DEVICES, 2)]
    up_between = [(i, i + 1) for i in range(1, DEVICES - 1, 2)]
    scratch = [pltpu.VMEM((CHANS, CELLS), F32), pltpu.SemaphoreType.DMA((COARSEN + 1,))]

    from_odd, *kept = kernel_call(
        functools.partial(first_sweep, True),
        [narrow, *held],
        [inputs, guess, weights],
        "first_sweep_odd",
        4,
        hbm=(0, 1, 2),
        scratch=scratch,
    )
    left_even = send(from_odd, up_between)
    from_even, own_w, later_w, start = kernel_call(
        functools.partial(first_sweep, False),
        [narrow, *held],
        [inputs, guess, weights, *kept, from_odd],
        "first_sweep_even",
        4,
        hbm=(0, 1, 2),
        scratch=scratch,
        aliases={3: 1, 4: 2, 5: 3},
    )
    left_odd = send(from_even, up_inside)
    even_w = send(own_w, up_inside)

    left_even, start = kernel_call(
        in_order, [narrow, wide], [left_even, start], "even_first", 1, aliases={0: 0, 1: 1}
    )
    rhs, solved, c1 = kernel_call(
        second_sweep_lead,
        [wide, wide, narrow],
        [left_odd, own_w, later_w, start],
        "second_sweep_lead",
        40,
    )
    got3 = send(c1, [(1, 3)])
    rhs_of_even, first, start, solved, sent = kernel_call(
        second_sweep_even,
        [wide, wide, wide, wide, narrow],
        [left_even, own_w, later_w, inputs, start, solved],
        "second_sweep_even",
        4,
        hbm=(3,),
        scratch=[pltpu.VMEM((CHANS, CELLS), F32), pltpu.SemaphoreType.DMA(())],
        aliases={4: 2, 5: 3},
    )
    even_rhs = send(sent, up_inside)
    first = send(first, [(4, 5), (8, 9)])
    rhs, solved = kernel_call(
        second_sweep_odd,
        [wide, wide],
        [left_odd, own_w, later_w, rhs, solved],
        "second_sweep_odd",
        0,
        aliases={3: 0, 4: 1},
    )
    both = [even_rhs, rhs, even_w, own_w]

    def chained(body, args, name, steps, out=narrow):
        nonlocal solved
        value, solved = kernel_call(
            body, [out, wide], [*args, solved], name, steps, aliases={len(args): 1}
        )
        return value

    def pair(owners, keep, got, name):
        return chained(functools.partial(two_steps, owners, keep), [*both, got], name, 2)

    part = chained(lead_half, [got3, even_w], "lead_first", 7, wide)
    upper1 = chained(lead_rest, [rhs, own_w, even_rhs, part], "relax_lead", 20)
    got4 = send(upper1, [(3, 5)])
    c5 = chained(functools.partial(one_step, (5, 9)), [first, rhs, own_w], "relax_first", 1)
    got3_rest = send(c5, [(5, 7)])
    got3_last = send(c5, [(9, 11)])
    c5_lead = pair((5,), False, got4, "again_lead")
    got5 = send(c5_lead, [(5, 7)])
    upper7 = pair((7,), False, got3_rest, "relax_rest")
    got4_rest = send(upper7, [(7, 9)])
    upper_prev = send(upper7, [(7, 11)])
    z2 = pair((7,), True, got5, "again_end_lead")
    got6 = send(z2, [(7, 11)])
    got4_rest, solved = kernel_call(
        in_order, [narrow, wide], [got4_rest, solved], "upper_first", 10, aliases={0: 0, 1: 1}
    )
    upper11 = chained(
        functools.partial(steps_or_copy, 11, 7), [z2, *both, got3_last], "relax_last", 2
    )
    got6_rest = send(upper11, [(7, 9), (11, 15)])
    c9 = chained(
        functools.partial(steps_or_copy, 9, 11), [upper11, *both, got4_rest], "again_rest", 2
    )
    got5_rest = send(c9, [(9, 11), (11, 13)])
    base = chained(coarse_base, [upper_prev, own_w], "coarse_base", 1, wide)
    base = chained(lead_base, [base, own_w, got6], "lead_base", 2, wide)
    z3 = chained(again_end, [*both, base, got3, got4, z2, got5_rest], "again_end_rest", 2)
    got7 = send(z3, [(11, 13), (13, 15)])
    got7b = send(z3, [(11, 15), (3, 2), (5, 4), (7, 8)])
    c13 = chained(lead_two_steps, [z3, got5, *both, got6_rest, got7], "final_lead", 2)
    got8 = send(c13, [(13, 15), (9, 11)])
    got8b = send(c13, [(13, 14), (9, 10), (11, 12), (7, 6)])
    (solved,) = kernel_call(
        end_step, [wide], [got6_rest, *both, got7, got7b, solved], "coarse_end", 4, aliases={7: 0}
    )
    return kernel_call(
        last_sweep,
        [jax.ShapeDtypeStruct((COARSEN, CHANS, CELLS), F32)],
        [start, got8b, got8, got3, got4, got5, got6_rest, got7, got7b, *both, rhs_of_even, later_w, solved],
        "last_sweep",
        4,
        scratch=[
            pltpu.VMEM(STATE, F32),
            pltpu.VMEM((COARSEN, CHANS, CELLS), F32),
            pltpu.SemaphoreType.DMA((COARSEN,)),
        ],
    )[0]


def solution(mesh):
    return jax.shard_map(
        per_device,
        mesh=mesh,
        in_specs=(P(None, "batch"), P("layer", None, "batch"), P("layer", None, None)),
        out_specs=P("layer", None, "batch"),
        check_vma=False,
    )
```
